256 devices in a mesh: seq: 16 (over x, y), grp: 8 (over z_hi, core), rep: 2 (over z_lo).
Axes of the slice: x: 4, y: 4, z: 8 (z_hi: 4, z_lo: 2; z = z_hi * 2 + z_lo), core: 2. Of those that a mesh axis runs over, the one named last changes fastest.
Arguments:
- latents: bfloat16 [2, 2048, 2560], P('rep', 'seq'), may hold values from -6 to 6
- noise_draw: bfloat16 [2, 2048, 2560], P('rep', 'seq'), may hold values from -6 to 6
- timesteps: float32 [2], P('rep'), may hold values from 0.2 to 0.9
- gen_gain: float32 [2560], replicated, may hold values from 0.5 to 1.5
- up_weight: bfloat16 [2560, 6912], P(None, 'grp'), may hold values from -0.125 to 0.125
- down_weight: bfloat16 [2560, 6912], P(None, 'grp'), may hold values from -0.078125 to 0.078125
- score_gain: float32 [2560], replicated, may hold values from 0.5 to 1.5
- qkv_weight: bfloat16 [2560, 3, 3072], P('seq', None, 'grp'), may hold values from -1 to 1
- out_weight: bfloat16 [2560, 3072], P('seq', 'grp'), may hold values from -0.109375 to 0.109375
- query_down: bfloat16 [2560, 64], P('seq'), may hold values from -0.125 to 0.125
- query_up: bfloat16 [64, 3072], P(None, 'grp'), may hold values from -0.375 to 0.375
- output_down: bfloat16 [3072, 64], P('grp'), may hold values from -0.109375 to 0.109375
- output_up: bfloat16 [64, 2560], replicated, may hold values from -0.5 to 0.5
Outputs:
- sample: bfloat16 [2, 2048, 2560], P('rep', 'seq', 'grp')
- up_weight_gradient: float32 [2560, 6912], P(('seq', 'rep'), 'grp')
- down_weight_gradient: float32 [2560, 6912], P(('seq', 'rep'), 'grp')
- adapter_up_gradient: float32 [64, 2560], P(('seq', 'rep'), 'grp')
The draws below stay inside these ranges and needn't reach their ends.
All inputs are finite; a program needn't handle non-finite values.
Results may differ from the reference program's by a relative error of at most 0.035.
Values may be sent and summed in bfloat16 or wider, within the bound.
No kernel may reach another device: no remote copies, remote signals or barrier semaphores. Data moves between devices by JAX's collectives and lax.ppermute only.
A program may use at most 128 MiB of HBM per device.

```python
import jax
import jax.numpy as jnp
from jax import lax

MODEL_CHANNELS = 2560
FF = 6912
HEADS = 24
HEAD = 128
ADAPTER_DEPTH = 64
TOKENS = 2048
CLIPS = 2


def token_rows(key, own_number):
    own_key = jax.random.fold_in(key, own_number)
    values = jax.random.normal(own_key, (CLIPS, TOKENS, MODEL_CHANNELS), jnp.float32)
    return jnp.clip(values, -6.0, 6.0).astype(jnp.bfloat16)


def draw_latents(key, part):
    return token_rows(key, 11)


def draw_noise_draw(key, part):
    return token_rows(key, 12)


def draw_qkv_weight(key, part):
    own_key = jax.random.fold_in(key, 13)
    width = HEADS * HEAD
    values = jax.random.normal(own_key, (MODEL_CHANNELS, 3, width), jnp.float32) * MODEL_CHANNELS ** (-0.5)
    return jnp.clip(values, -1.0, 1.0).astype(jnp.bfloat16)


def level_of(rng, extent, pieces, least, high):
    def one(position, blocks):
        heights = jax.random.uniform(jax.random.fold_in(jax.random.fold_in(rng, 6), position), (blocks,), jnp.float32, least / len(pieces), high / len(pieces))
        return jnp.repeat(jnp.exp(heights), extent[position] // blocks).reshape((-1,) + (1,) * (len(extent) - position - 1))

    factor_of = one(*pieces[0])
    for cut in pieces[1:]:
        factor_of = factor_of * one(*cut)
    return factor_of


def bell_draw(key, shape, scale, limit, shards=(), kind=jnp.bfloat16):
    result = scale * jax.random.normal(key, shape, jnp.float32)
    if shards:
        result = result * level_of(key, shape, shards, -0.22, 0.18)
    return jnp.clip(result, -limit, limit).astype(kind)


def setup_inputs(seed: int = 0) -> dict:
    seeds = jax.random.split(jax.random.key(seed), 14)
    return {
        "latents": draw_latents(jax.random.fold_in(seeds[13], 71), 0),
        "noise_draw": draw_noise_draw(jax.random.fold_in(seeds[13], 71), 0),
        "timesteps": jnp.clip(0.2 + 0.7 * jax.random.uniform(seeds[2], (CLIPS,), jnp.float32) ** level_of(seeds[2], (CLIPS,), ((0, 2),), -0.2, 0.2), 0.2, 0.9),
        "gen_gain": jnp.clip(1.0 + 0.1 * jax.random.normal(seeds[3], (MODEL_CHANNELS,), jnp.float32), 0.5, 1.5),
        "up_weight": bell_draw(seeds[4], (MODEL_CHANNELS, FF), MODEL_CHANNELS ** -0.5, 0.125, ((1, 8),)),
        "down_weight": bell_draw(seeds[5], (MODEL_CHANNELS, FF), FF ** -0.5, 0.078125, ((1, 8),)),
        "score_gain": jnp.clip(1.0 + 0.1 * jax.random.normal(seeds[6], (MODEL_CHANNELS,), jnp.float32), 0.5, 1.5),
        "qkv_weight": draw_qkv_weight(jax.random.fold_in(seeds[13], 71), 0),
        "out_weight": bell_draw(seeds[8], (MODEL_CHANNELS, HEADS * HEAD), (HEADS * HEAD) ** -0.5, 0.109375, ((0, 16), (1, 8))),
        "query_down": bell_draw(seeds[9], (MODEL_CHANNELS, ADAPTER_DEPTH), MODEL_CHANNELS ** -0.5, 0.125, ((0, 16),)),
        "query_up": bell_draw(seeds[10], (ADAPTER_DEPTH, HEADS * HEAD), (4 * ADAPTER_DEPTH) ** -0.5, 0.375, ((1, 8),)),
        "output_down": bell_draw(seeds[11], (HEADS * HEAD, ADAPTER_DEPTH), (HEADS * HEAD) ** -0.5, 0.109375, ((0, 8),)),
        "output_up": bell_draw(seeds[12], (ADAPTER_DEPTH, MODEL_CHANNELS), (2 * ADAPTER_DEPTH) ** -0.5, 0.5),
    }


def normalize(values, gain_vector):
    widened = values.astype(jnp.float32)
    return widened * lax.rsqrt(lax.optimization_barrier(jnp.mean(widened * widened, axis=-1, keepdims=True)) + 1e-06) * gain_vector.astype(jnp.float32)

def gelu_tanh(values):
    return jax.nn.gelu(values, approximate=True)

def split_heads(matrix):
    return matrix.reshape(matrix.shape[0], HEADS, HEAD).transpose(1, 0, 2)

def attend(queries, key_heads, value_heads):
    score_scale = HEAD ** (-0.5)

    def one_head(triple):
        query_head, key_head, value_head = triple
        scores = jnp.dot(query_head, key_head.T, preferred_element_type=jnp.float32) * score_scale
        row_top = lax.optimization_barrier(jnp.max(scores, axis=-1, keepdims=True))
        weights = jnp.exp(scores - row_top)
        row_total = lax.optimization_barrier(jnp.sum(weights, axis=-1, keepdims=True))
        mixed_rows = jnp.dot(weights.astype(jnp.bfloat16), value_head, preferred_element_type=jnp.float32)
        return mixed_rows / row_total
    outputs = lax.map(one_head, (queries, key_heads, value_heads))
    return outputs.transpose(1, 0, 2).reshape(queries.shape[1], HEADS * HEAD).astype(jnp.bfloat16)

def contracted_rows(left_rows, right_rows, precision=None):
    return lax.dot_general(left_rows, right_rows, (((0,), (0,)), ((), ())), preferred_element_type=jnp.float32, precision=precision)

def reference(latents, noise_draw, timesteps, gen_gain, up_weight, down_weight, score_gain, qkv_weight, out_weight, query_down, query_up, output_down, output_up):
    head_cols = HEADS * HEAD
    back_dims = (((1,), (1,)), ((), ()))
    sample_batch = []
    up_weight_gradient = jnp.zeros((MODEL_CHANNELS, FF), jnp.float32)
    down_weight_gradient = jnp.zeros((MODEL_CHANNELS, FF), jnp.float32)
    adapter_up_gradient = jnp.zeros((ADAPTER_DEPTH, MODEL_CHANNELS), jnp.float32)
    for clip_index in range(CLIPS):
        latent = latents[clip_index]
        normed = normalize(latent, gen_gain).astype(jnp.bfloat16)
        hidden_pre = jnp.dot(normed, up_weight, preferred_element_type=jnp.float32)
        hidden = gelu_tanh(hidden_pre).astype(jnp.bfloat16)
        update = lax.dot_general(hidden, down_weight, back_dims, preferred_element_type=jnp.float32)
        sample = (latent.astype(jnp.float32) + update).astype(jnp.bfloat16)
        sample_batch.append(sample)
        clip_time = timesteps[clip_index]
        noise_rows = noise_draw[clip_index].astype(jnp.float32)
        noisy_rows = ((1.0 - clip_time) * sample.astype(jnp.float32) + clip_time * noise_rows).astype(jnp.bfloat16)
        score_in = normalize(noisy_rows, score_gain).astype(jnp.bfloat16)
        projected = jnp.dot(score_in, qkv_weight.reshape(MODEL_CHANNELS, 3 * head_cols), preferred_element_type=jnp.float32)
        query_real = projected[:, :head_cols].astype(jnp.bfloat16)
        key_rows = projected[:, head_cols:2 * head_cols].astype(jnp.bfloat16)
        value_rows = projected[:, 2 * head_cols:].astype(jnp.bfloat16)
        query_low = jnp.dot(score_in, query_down, preferred_element_type=jnp.float32).astype(jnp.bfloat16)
        query_fake = (projected[:, :head_cols] + jnp.dot(query_low, query_up, preferred_element_type=jnp.float32)).astype(jnp.bfloat16)
        key_heads = split_heads(key_rows)
        value_heads = split_heads(value_rows)
        mixed_real = attend(split_heads(query_real), key_heads, value_heads)
        mixed_fake = attend(split_heads(query_fake), key_heads, value_heads)
        velocity_real = lax.dot_general(mixed_real, out_weight, back_dims, preferred_element_type=jnp.float32)
        fake_latent_rows = jnp.dot(mixed_fake, output_down, preferred_element_type=jnp.float32)
        velocity_fake = lax.dot_general(mixed_fake, out_weight, back_dims, preferred_element_type=jnp.float32) + jnp.dot(fake_latent_rows, output_up.astype(jnp.float32), precision=lax.Precision.HIGHEST)
        cotangent = (clip_time * (velocity_real - velocity_fake)).astype(jnp.bfloat16)
        fake_score_error = velocity_fake - (noise_rows - sample.astype(jnp.float32))
        hidden_grad = jnp.dot(cotangent, down_weight, preferred_element_type=jnp.float32)
        _, backward = jax.vjp(gelu_tanh, hidden_pre)
        pre_grad = backward(hidden_grad)[0].astype(jnp.bfloat16)
        up_weight_gradient = up_weight_gradient + contracted_rows(normed, pre_grad)
        down_weight_gradient = down_weight_gradient + contracted_rows(cotangent, hidden)
        adapter_up_gradient = adapter_up_gradient + contracted_rows(fake_latent_rows, fake_score_error, lax.Precision.HIGHEST)
    return (jnp.stack(sample_batch), up_weight_gradient, down_weight_gradient, adapter_up_gradient)
```

```python
import jax
import jax.numpy as jnp
from jax import lax
from jax.sharding import PartitionSpec as P

HEAD = 128
F32 = jnp.float32
BF16 = jnp.bfloat16


def normalize(values, gain_vector):
    widened = values.astype(F32)
    return (
        widened
        * lax.rsqrt(jnp.mean(widened * widened, axis=-1, keepdims=True) + 1e-06)
        * gain_vector
    )


def gelu_tanh(values):
    return jax.nn.gelu(values, approximate=True)


def contracted_rows(left_rows, right_rows, precision=None):
    return lax.dot_general(
        left_rows,
        right_rows,
        (((0,), (0,)), ((), ())),
        preferred_element_type=F32,
        precision=precision,
    )


def move_x(d):
    return "seq", [(x * 4 + y, ((x + d) % 4) * 4 + y) for x in range(4) for y in range(4)]


def move_y(d):
    return "seq", [(x * 4 + y, x * 4 + (y + d) % 4) for x in range(4) for y in range(4)]


def move_z(d):
    return "grp", [(z * 2 + c, ((z + d) % 4) * 2 + c) for z in range(4) for c in range(2)]


CORE = ("grp", [(z * 2 + c, z * 2 + 1 - c) for z in range(4) for c in range(2)])
REP = ("rep", [(0, 1), (1, 0)])


def send(values, route):
    return lax.ppermute(values, route[0], route[1])


def ring_gather(values, move):
    return [values, send(values, move(-1)), send(values, move(2)), send(values, move(1))]


def ring_gather_parts(values, move):
    up = send(values, move(-1))
    down = send(values, move(1))
    half = values.shape[0] // 2
    first = send(down[:half], move(1))
    second = send(up[half:], move(-1))
    return up, first, second, down


def ring_exchange(block_of, move):
    return [
        block_of(0),
        send(block_of(3), move(3)),
        send(block_of(2), move(2)),
        send(block_of(1), move(1)),
    ]


def ring_sum(block_of, move):
    arrived = [send(block_of(k).astype(BF16), move(k)) for k in (1, 2, 3)]
    total = block_of(0)
    for piece in arrived:
        total = total + piece.astype(F32)
    return total


def group_sum(values):
    blocks = values.reshape(4, 2, 16, values.shape[-1])
    other = send(blocks[:, 1].astype(BF16), CORE)
    pair = blocks[:, 0] + other.astype(F32)
    return ring_sum(lambda k: pair[k], move_z)


def group_gather(rows):
    column = jnp.stack(ring_gather(rows, move_z))
    other = send(column, CORE)
    return jnp.stack([column, other], axis=1).reshape(128, rows.shape[-1])


def shards(
    latents,
    noise_draw,
    timesteps,
    gen_gain,
    up_weight,
    down_weight,
    score_gain,
    qkv_weight,
    out_weight,
    query_down,
    query_up,
    output_down,
    output_up,
):
    place = lax.axis_index("seq")
    at_x, at_y = place // 4, place % 4
    group = lax.axis_index("grp")
    at_z, at_core = group // 2, group % 2
    at_rep = lax.axis_index("rep")
    clip_time = timesteps[0]
    back_dims = (((1,), (1,)), ((), ()))
    width = latents.shape[2]
    share = width // 8
    head_width = out_weight.shape[1]

    def relative_rows(values):
        return jnp.concatenate(
            [
                lax.dynamic_slice_in_dim(
                    values, ((at_z + dz) % 4 * 2 + (at_core + dc) % 2) * 16, 16, 0
                )
                for dz in range(4)
                for dc in range(2)
            ]
        )

    def absolute_rows(values):
        return jnp.concatenate(
            [
                lax.dynamic_slice_in_dim(
                    values, ((z + 4 - at_z) % 4 * 2 + (c + at_core) % 2) * 16, 16, 0
                )
                for z in range(4)
                for c in range(2)
            ]
        )

    own = jnp.concatenate(
        [qkv_weight.reshape(qkv_weight.shape[0], 3 * head_width), query_down], axis=1
    )
    columns = own.shape[1]
    half = own.shape[0] // 2
    quarter = half // 2
    full = jnp.zeros((4, 4, 2, half, columns), BF16)
    parts = []
    for which, (first_move, second_move, first_at, second_at) in enumerate(
        ((move_x, move_y, at_x, at_y), (move_y, move_x, at_y, at_x))
    ):
        mine = own[which * half : (which + 1) * half]
        up, opp_a, opp_b, down = ring_gather_parts(mine, first_move)
        line = jnp.zeros((4, half, columns), BF16)
        line = lax.dynamic_update_slice(line, mine[None], (first_at, 0, 0))
        line = lax.dynamic_update_slice(line, up[None], ((first_at + 1) % 4, 0, 0))
        line = lax.dynamic_update_slice(line, down[None], ((first_at + 3) % 4, 0, 0))
        line = lax.dynamic_update_slice(line, opp_a[None], ((first_at + 2) % 4, 0, 0))
        line = lax.dynamic_update_slice(line, opp_b[None], ((first_at + 2) % 4, quarter, 0))
        up, opp_a, opp_b, down = ring_gather_parts(line, second_move)
        parts.append((line, up, opp_a, opp_b, down))
    line, up, opp_a, opp_b, down = parts[0]
    for piece, x0, distance in (
        (line, 0, 0),
        (up, 0, 1),
        (down, 0, 3),
        (opp_a, 0, 2),
        (opp_b, 2, 2),
    ):
        full = lax.dynamic_update_slice(
            full, piece[:, None, None], (x0, (at_y + distance) % 4, 0, 0, 0)
        )
    line, up, opp_a, opp_b, down = parts[1]
    for piece, y0, distance in (
        (line, 0, 0),
        (up, 0, 1),
        (down, 0, 3),
        (opp_a, 0, 2),
        (opp_b, 2, 2),
    ):
        full = lax.dynamic_update_slice(
            full, piece[None, :, None], ((at_x + distance) % 4, y0, 1, 0, 0)
        )
    score_weight = full.reshape(width, columns)

    latent = relative_rows(latents[0])
    noise_rows = relative_rows(noise_draw[0]).astype(F32)
    normed = normalize(latent, gen_gain).astype(BF16)
    hidden_pre = jnp.dot(normed, up_weight, preferred_element_type=F32)
    hidden = gelu_tanh(hidden_pre).astype(BF16)
    update = group_sum(
        lax.dot_general(hidden, down_weight, back_dims, preferred_element_type=F32)
    )
    sample = group_gather((latent[:16].astype(F32) + update).astype(BF16))
    sample_share = lax.dynamic_slice_in_dim(sample, group * share, share, 1)
    noise_share = lax.dynamic_slice_in_dim(noise_rows, group * share, share, 1)
    noisy_rows = (
        (1.0 - clip_time) * sample.astype(F32) + clip_time * noise_rows
    ).astype(BF16)
    score_in = normalize(noisy_rows, score_gain).astype(BF16)

    projected = jnp.dot(score_in, score_weight, preferred_element_type=F32)
    query_wide = projected[:, :head_width]
    key_rows = projected[:, head_width : 2 * head_width].astype(BF16)
    value_rows = projected[:, 2 * head_width : 3 * head_width].astype(BF16)
    query_low = projected[:, 3 * head_width :].astype(BF16)

    def spread(values, first_move, second_move, axis):
        up, opp_a, opp_b, down = ring_gather_parts(values, first_move)
        line = jnp.stack([values, up, jnp.concatenate([opp_a, opp_b]), down])
        up, opp_a, opp_b, down = ring_gather_parts(line, second_move)
        return jnp.stack([line, up, jnp.concatenate([opp_a, opp_b]), down], axis=axis)

    tokens = 16 * key_rows.shape[0]
    keys = spread(key_rows, move_x, move_y, 0).reshape(tokens, head_width)
    values = spread(value_rows, move_y, move_x, 1).reshape(tokens, head_width)

    query_fake = (
        query_wide + jnp.dot(query_low, query_up, preferred_element_type=F32)
    ).astype(BF16)
    queries = jnp.concatenate([query_wide.astype(BF16), query_fake])
    mixed = []
    for start in range(0, head_width, HEAD):
        cut = slice(start, start + HEAD)
        scores = lax.dot_general(
            queries[:, cut], keys[:, cut], back_dims, preferred_element_type=F32
        ) * (HEAD ** (-0.5))
        weights = jnp.exp(scores - jnp.max(scores, axis=-1, keepdims=True))
        total = jnp.sum(weights, axis=-1, keepdims=True)
        mixed.append(
            jnp.dot(weights.astype(BF16), values[:, cut], preferred_element_type=F32) / total
        )
    mixed = jnp.concatenate(mixed, axis=1).astype(BF16)
    mixed_real, mixed_fake = mixed[:128], mixed[128:]

    out_rows = lax.all_gather(out_weight, "seq", axis=0, tiled=True)

    def by_y(rows):
        return (
            rows.reshape(4, 4, width // 16, rows.shape[1])
            .transpose(1, 0, 2, 3)
            .reshape(width, rows.shape[1])
        )

    out_rows = by_y(out_rows)
    up_columns = by_y(output_up.T)
    latent_part = jnp.dot(mixed_fake, output_down, preferred_element_type=F32)
    difference = (
        lax.dot_general(mixed_real, out_rows, back_dims, preferred_element_type=F32)
        - lax.dot_general(mixed_fake, out_rows, back_dims, preferred_element_type=F32)
        - lax.dot_general(
            latent_part, up_columns.astype(F32), back_dims, precision=lax.Precision.HIGHEST
        )
    )
    summed = group_sum(jnp.concatenate([difference, latent_part], axis=1))
    gathered = group_gather(
        jnp.concatenate([clip_time * summed[:, :width], summed[:, width:]], axis=1).astype(BF16)
    )
    cotangent, fake_latent = gathered[:, :width], gathered[:, width:]

    hidden_grad = jnp.dot(cotangent, by_y(down_weight), preferred_element_type=F32)
    _, backward = jax.vjp(gelu_tanh, hidden_pre)
    pre_grad = backward(hidden_grad)[0].astype(BF16)

    late_hidden, late_normed, _ = lax.optimization_barrier((hidden, normed, queries))
    block = width // 4

    def split_over(values, at):
        return lambda k: lax.dynamic_slice_in_dim(values, (at + k) % 4 * block, block, 1)

    def finish(term, at, move):
        blocks = term.reshape(4, width // 16, term.shape[1])
        total = ring_sum(
            lambda k: lax.dynamic_index_in_dim(blocks, (at + k) % 4, 0, keepdims=False), move
        )
        rows = total.shape[0] // 2
        kept = lax.dynamic_slice_in_dim(total, at_rep * rows, rows, 0)
        given = lax.dynamic_slice_in_dim(total, (1 - at_rep) * rows, rows, 0)
        return kept + send(given.astype(BF16), REP).astype(F32)

    hidden_line = jnp.concatenate(ring_gather(late_hidden, move_y))
    cotangent_line = jnp.concatenate(ring_exchange(split_over(cotangent, at_y), move_y))
    down_weight_gradient = finish(contracted_rows(cotangent_line, hidden_line), at_x, move_x)

    normed_line = jnp.concatenate(ring_exchange(split_over(late_normed, at_x), move_x))
    pre_line = jnp.concatenate(ring_gather(pre_grad, move_x))
    up_weight_gradient = finish(contracted_rows(normed_line, pre_line), at_y, move_y)

    wide = jnp.concatenate(
        [
            mixed_fake.astype(F32),
            sample_share.astype(F32) - noise_share,
            fake_latent.astype(F32),
        ],
        axis=1,
    )
    moments = contracted_rows(fake_latent.astype(F32), wide, lax.Precision.HIGHEST)

    def rows_sum(term, at, move):
        blocks = term.reshape(4, term.shape[0] // 4, term.shape[1])
        return ring_sum(
            lambda k: lax.dynamic_index_in_dim(blocks, (at + k) % 4, 0, keepdims=False), move
        )

    moments = rows_sum(rows_sum(moments, at_x, move_x), at_y, move_y)
    kept = lax.dynamic_slice_in_dim(moments, at_rep * 2, 2, 0)
    given = lax.dynamic_slice_in_dim(moments, (1 - at_rep) * 2, 2, 0)
    moments = kept + send(given.astype(BF16), REP).astype(F32)
    through_out = lax.dot_general(
        moments[:, :head_width],
        out_rows.astype(F32),
        back_dims,
        precision=lax.Precision.HIGHEST,
    )
    through_out = (
        through_out.reshape(2, 4, 4, width // 16)
        .transpose(2, 1, 0, 3)
        .reshape(4, 2, 2, 2, width // 16)
        .transpose(0, 1, 3, 2, 4)
        .reshape(4, 2, 2, share)
    )
    other = send(
        lax.dynamic_index_in_dim(through_out, 1 - at_core, 1, keepdims=False).astype(BF16), CORE
    )
    pair = lax.dynamic_index_in_dim(through_out, at_core, 1, keepdims=False) + other.astype(F32)
    through_out = ring_sum(
        lambda k: lax.dynamic_index_in_dim(pair, (at_z + k) % 4, 0, keepdims=False), move_z
    )
    up_share = lax.dynamic_slice_in_dim(output_up, group * share, share, 1)
    adapter_up_gradient = (
        through_out
        + moments[:, head_width : head_width + share]
        + jnp.dot(
            moments[:, head_width + share :],
            up_share.astype(F32),
            precision=lax.Precision.HIGHEST,
        )
    )
    return (
        absolute_rows(sample_share)[None],
        up_weight_gradient,
        down_weight_gradient,
        adapter_up_gradient,
    )


def solution(mesh):
    in_specs = (
        P("rep", "seq", None),
        P("rep", "seq", None),
        P("rep"),
        P(),
        P(None, "grp"),
        P(None, "grp"),
        P(),
        P("seq", None, "grp"),
        P("seq", "grp"),
        P("seq", None),
        P(None, "grp"),
        P("grp", None),
        P(),
    )
    out_specs = (
        P("rep", "seq", "grp"),
        P(("seq", "rep"), "grp"),
        P(("seq", "rep"), "grp"),
        P(("seq", "rep"), "grp"),
    )
    return jax.shard_map(shards, mesh=mesh, in_specs=in_specs, out_specs=out_specs, check_vma=False)
```

```python
import jax
import jax.numpy as jnp
from jax import lax
from jax.experimental import pallas as pl
from jax.experimental.pallas import tpu as pltpu
from jax.sharding import PartitionSpec as P

HEAD = 128
F32 = jnp.float32
BF16 = jnp.bfloat16


def move_x(d):
    return "seq", [(x * 4 + y, ((x + d) % 4) * 4 + y) for x in range(4) for y in range(4)]


def move_y(d):
    return "seq", [(x * 4 + y, x * 4 + (y + d) % 4) for x in range(4) for y in range(4)]


def move_z(d):
    return "grp", [(z * 2 + c, ((z + d) % 4) * 2 + c) for z in range(4) for c in range(2)]


def to_heads(d):
    return "seq", [pair for pair in move_x(d)[1] if pair[1] // 4 < 3]


def from_heads(d):
    return "seq", [pair for pair in move_x(d)[1] if pair[0] // 4 < 3]


CORE = ("grp", [(z * 2 + c, z * 2 + 1 - c) for z in range(4) for c in range(2)])
REP = ("rep", [(0, 1), (1, 0)])


def send(values, route):
    return lax.ppermute(values, route[0], route[1])


def ring_gather(values, move):
    return [values, send(values, move(-1)), send(values, move(2)), send(values, move(1))]


def ring_gather_parts(values, move):
    up = send(values, move(-1))
    down = send(values, move(1))
    half = values.shape[0] // 2
    first = send(down[:half], move(1))
    second = send(up[half:], move(-1))
    return up, first, second, down


def ring_exchange(block_of, move):
    return [
        block_of(0),
        send(block_of(3), move(3)),
        send(block_of(2), move(2)),
        send(block_of(1), move(1)),
    ]


def ring_sum(block_of, move):
    arrived = [send(block_of(k).astype(BF16), move(k)) for k in (1, 2, 3)]
    total = block_of(0)
    for piece in arrived:
        total = total + piece.astype(F32)
    return total


NN = (((1,), (0,)), ((), ()))
NT = (((1,), (1,)), ((), ()))
TN = (((0,), (0,)), ((), ()))


def product(left, right, dims):
    return lax.dot_general(left, right, dims, preferred_element_type=F32)


def in_vmem():
    return pl.BlockSpec(memory_space=pltpu.VMEM)


def in_smem():
    return pl.BlockSpec(memory_space=pltpu.SMEM)


def anywhere():
    return pl.BlockSpec(memory_space=pl.ANY)


def fetch(sems, *pairs):
    copies = [
        pltpu.make_async_copy(source, target, sems.at[i])
        for i, (source, target) in enumerate(pairs)
    ]
    for copy in copies:
        copy.start()
    return copies


def call(kernel, operands, specs, outs, scratch=(), flops=0, mib=16):
    moved = sum(a.size * a.dtype.itemsize for a in operands)
    return pl.pallas_call(
        kernel,
        out_shape=[jax.ShapeDtypeStruct(shape, kind) for shape, kind in outs],
        in_specs=specs,
        out_specs=[in_vmem() for _ in outs],
        scratch_shapes=list(scratch),
        cost_estimate=pl.CostEstimate(flops=flops, bytes_accessed=moved, transcendentals=0),
        compiler_params=pltpu.CompilerParams(vmem_limit_bytes=mib * 1024 * 1024),
    )(*operands)


def unit_rows(values, gain):
    scale = lax.rsqrt(jnp.mean(values * values, axis=-1, keepdims=True) + 1e-06)
    return values * scale * gain


def generator_kernel(at, latent_ref, gain_ref, up_ref, normed_ref, hidden_ref, slope_ref):
    for dz in range(4):
        for dc in range(2):
            block = lax.rem(at[2] + dz, 4) * 2 + lax.rem(at[3] + dc, 2)
            start = pl.multiple_of(block * 16, 16)
            values = latent_ref[pl.ds(start, 16), :].astype(F32)
            first = (dz * 2 + dc) * 16
            normed_ref[first : first + 16, :] = unit_rows(values, gain_ref[...]).astype(BF16)
    pre = product(normed_ref[...], up_ref[...], NT)
    curve = jnp.tanh(0.7978845608028654 * (pre + 0.044715 * (pre * pre * pre)))
    hidden_ref[...] = (0.5 * pre * (1.0 + curve)).astype(BF16)
    slope_ref[...] = 0.5 * (1.0 + curve) + 0.5 * pre * (1.0 - curve * curve) * (
        0.7978845608028654 * (1.0 + 0.134145 * (pre * pre))
    )


def update_kernel(hidden_ref, down_ref, own_ref, other_ref):
    update = product(hidden_ref[...], down_ref[...], NN)
    for dz in range(4):
        own_ref[dz] = update[dz * 32 : dz * 32 + 16]
        other_ref[dz] = update[dz * 32 + 16 : dz * 32 + 32].astype(BF16)


def strips_kernel(normed_ref, out_ref):
    for y in range(4):
        for x in range(4):
            out_ref[y, :, x * 160 : (x + 1) * 160] = normed_ref[
                :, x * 640 + y * 160 : x * 640 + (y + 1) * 160
            ]


def score_kernel(
    at, time, update_ref, latent_ref, noise_ref, gain_ref, quarters_ref, strips_ref
):
    start = pl.multiple_of((at[2] * 2 + at[3]) * 16, 16)
    latent = latent_ref[pl.ds(start, 16), :].astype(F32)
    noise = noise_ref[pl.ds(start, 16), :].astype(F32)
    sample = (latent + update_ref[...]).astype(BF16)
    noisy = ((1.0 - time[0]) * sample.astype(F32) + time[0] * noise).astype(BF16).astype(F32)
    score = unit_rows(noisy, gain_ref[...]).astype(BF16)
    for x in range(4):
        quarters_ref[x] = score[:, x * 640 : (x + 1) * 640]
    for g in range(8):
        strips_ref[g] = sample[:, g * 320 : (g + 1) * 320]


def project_kernel(at, column_hbm, other_hbm, *rest):
    weights_hbm, outs = rest[:5], rest[5:9]
    rows_ref, weight_ref, result, sems = rest[9:]
    part = weights_hbm[0].shape[0]
    pairs = []
    for dx in range(4):
        for dz in range(4):
            for dc, source in ((0, column_hbm), (1, other_hbm)):
                target = dx * 128 + (dz * 2 + dc) * 16
                pairs.append(
                    (source.at[pl.ds((dz * 4 + dx) * 16, 16)], rows_ref.at[pl.ds(target, 16)])
                )
    for ref, distance, first in zip(weights_hbm, (0, 1, 2, 2, 3), (0, 0, 0, part // 2, 0)):
        start = pl.multiple_of(lax.rem(at[1] + distance, 4) * part + first, 16)
        pairs.append((ref, weight_ref.at[pl.ds(start, ref.shape[0])]))
    for copy in fetch(sems, *pairs):
        copy.wait()
    result[...] = product(rows_ref[...], weight_ref[...], NN)
    for k in range(4):
        head = jnp.minimum(lax.rem(at[0] + k, 4), 2)
        for p in range(4):
            if p < 3:
                lanes = pl.ds(pl.multiple_of(p * 384 + head * HEAD, HEAD), HEAD)
                target_lanes = slice(p * HEAD, (p + 1) * HEAD)
            else:
                lanes = slice(1152, 1216)
                target_lanes = slice(3 * HEAD, 3 * HEAD + 64)
            for j in range(4):
                source, target = (j + k) % 4 * 128, j * 128
                outs[k][target : target + 128, target_lanes] = result[
                    source : source + 128, lanes
                ].astype(outs[k].dtype)


def finish_kernel(at, own_ref, one_ref, three_ref, up_ref, pairs_ref, query_ref):
    result = own_ref[...] + one_ref[...].astype(F32) + three_ref[...].astype(F32)
    rows = result.shape[0]
    head = pl.ds(pl.multiple_of(jnp.minimum(at[0], 2) * HEAD, HEAD), HEAD)
    query = result[:, :HEAD]
    pairs_ref[...] = result[:, HEAD : 3 * HEAD].astype(BF16)
    low = result[:, 3 * HEAD :].astype(BF16)
    query_ref[:rows] = query.astype(BF16)
    query_ref[rows:] = (query + product(low, up_ref[:, head], NN)).astype(BF16)


def attention_kernel(query_ref, *rest):
    pieces, (mixed_ref, pairs_ref, sems) = rest[:4], rest[4:]
    count = pieces[0].shape[0]
    for copy in fetch(
        sems, *[(pieces[i], pairs_ref.at[pl.ds(i * count, count)]) for i in range(4)]
    ):
        copy.wait()
    for j in range(4):
        for which in range(2):
            first = which * count + j * 128
            scores = product(query_ref[first : first + 128, :], pairs_ref[:, :HEAD], NT)
            scores = scores * (HEAD ** (-0.5))
            weights = jnp.exp(scores - jnp.max(scores, axis=-1, keepdims=True))
            total = jnp.sum(weights, axis=-1, keepdims=True)
            mix = product(weights.astype(BF16), pairs_ref[:, HEAD:], NN) / total
            mixed_ref[j, which * 128 : (which + 1) * 128, :] = mix.astype(BF16)


def output_kernel(at, out_ref, down_ref, up_ref, *rest):
    pieces, (own_ref, other_ref, fake_ref, mixed) = rest[:4], rest[4:]
    for j in range(4):
        lanes = pl.ds(pl.multiple_of(lax.rem(at[0] + j, 4) * HEAD, HEAD), HEAD)
        mixed[:, lanes] = pieces[j][...]
    width = out_ref.shape[1]
    real, fake = mixed[:128, :width], mixed[128:, :width]
    fake_ref[...] = fake
    latent = product(fake, down_ref[...], NT)
    high = latent.astype(BF16)
    low = (latent - high.astype(F32)).astype(BF16)
    difference = (
        product(real, out_ref[...], NT)
        - product(fake, out_ref[...], NT)
        - (product(high, up_ref[...], NN) + product(low, up_ref[...], NN))
    )
    features = out_ref.shape[0]
    for dz in range(4):
        cut = slice(dz * 32, dz * 32 + 16)
        own_ref[dz, :, :features] = difference[cut]
        own_ref[dz, :, features:] = latent[cut]
        cut = slice(dz * 32 + 16, dz * 32 + 32)
        other_ref[dz, :, :features] = difference[cut].astype(BF16)
        other_ref[dz, :, features:] = latent[cut].astype(BF16)


def backward_kernel(
    column_hbm, other_hbm, down_ref, slope_ref, fake_ref, sample_ref, noise_ref,
    pre_ref, quarters_ref, both, whole, wide, sems,
):
    for copy in fetch(sems, (column_hbm, both.at[0]), (other_hbm, both.at[1])):
        copy.wait()
    features = down_ref.shape[1]
    quarter = features // 4
    for dz in range(4):
        for dc in range(2):
            cut = slice((dz * 2 + dc) * 16, (dz * 2 + dc) * 16 + 16)
            whole[cut, :] = both[dc, dz]
    for x in range(4):
        quarters_ref[x, :128, :] = whole[:, x * quarter : (x + 1) * quarter]
    latent = whole[:, features:]
    width, share, depth = fake_ref.shape[1], sample_ref.shape[1], latent.shape[1]
    error = sample_ref[...].astype(F32) - noise_ref[...].astype(F32)
    high = error.astype(BF16)
    wide[:, :width] = product(latent, fake_ref[...], TN)
    wide[:, width : width + share] = product(latent, high, TN) + product(
        latent, (error - high.astype(F32)).astype(BF16), TN
    )
    wide[:, width + share :] = product(latent, latent, TN)
    for x in range(4):
        quarters_ref[x, 128:144, :] = wide[x * 16 : x * 16 + 16, :quarter].astype(BF16)
        quarters_ref[x, 144:160, :] = jnp.zeros((16, quarter), BF16)
        quarters_ref[x, 144:160, : width + share + depth - quarter] = wide[
            x * 16 : x * 16 + 16, quarter:
        ].astype(BF16)
    grad = product(whole[:, :features], down_ref[...], NT)
    pre_ref[...] = (grad * slope_ref[...]).astype(BF16)


def term_kernel(at, *rest):
    lefts, rights = rest[:4], rest[4:8]
    outs, (left, right, term, sems) = rest[8:12], rest[12:]
    tall = left.shape[1]
    pairs = [(lefts[i], left.at[i]) for i in range(4)]
    pairs += [(rights[i], right.at[pl.ds(i * 128, 128)]) for i in range(4)]
    for copy in fetch(sems, *pairs):
        copy.wait()
    rows = jnp.concatenate([left[i, :128, :] for i in range(4)])
    term[...] = product(rows, right[...], TN)
    for k in range(4):
        start = pl.multiple_of(lax.rem(at[0] + k, 4) * 160, 16)
        outs[k][:160, :] = term[pl.ds(start, 160), :].astype(outs[k].dtype)
    if tall > 128:
        extra = left[0, 128:, :].astype(F32)
        for i in range(1, 4):
            extra = extra + left[i, 128:, :].astype(F32)
        for k in range(4):
            outs[k][160:, :] = jnp.zeros((16, outs[k].shape[1]), outs[k].dtype)
            outs[k][160:, :640] = extra[:16].astype(outs[k].dtype)
            outs[k][160:, 640:768] = extra[16:, :128].astype(outs[k].dtype)


def group_sum(own, other):
    pair = own + send(other, CORE).astype(F32)
    return ring_sum(lambda k: pair[k], move_z)


def group_gather(rows):
    column = jnp.stack(ring_gather(rows, move_z))
    return column, send(column, CORE)


def split_bf16(values):
    high = values.astype(BF16)
    return jnp.concatenate([high, (values - high.astype(F32)).astype(BF16)])


def shards(
    latents,
    noise_draw,
    timesteps,
    gen_gain,
    up_weight,
    down_weight,
    score_gain,
    qkv_weight,
    out_weight,
    query_down,
    query_up,
    output_down,
    output_up,
):
    place = lax.axis_index("seq")
    at_x, at_y = place // 4, place % 4
    group = lax.axis_index("grp")
    at_z, at_core = group // 2, group % 2
    at_rep = lax.axis_index("rep")
    at = jnp.stack([at_x, at_y, at_z, at_core]).astype(jnp.int32)
    clip_time = timesteps[0]
    rows, width = latents.shape[1:]
    units = up_weight.shape[1]
    share = width // 8
    head_width = out_weight.shape[1]
    depth = query_down.shape[1]
    vm, sm, hb = in_vmem(), in_smem(), anywhere()


    def relative_rows(values):
        return jnp.concatenate(
            [
                lax.dynamic_slice_in_dim(
                    values, ((at_z + dz) % 4 * 2 + (at_core + dc) % 2) * 16, 16, 0
                )
                for dz in range(4)
                for dc in range(2)
            ]
        )

    def pick(values, index):
        return lax.dynamic_index_in_dim(values, index % 4, 0, keepdims=False)

    own_weight = jnp.concatenate(
        [qkv_weight[:, 0], qkv_weight[:, 1], qkv_weight[:, 2], query_down], axis=1
    )
    columns = own_weight.shape[1]
    weight_up, weight_down = send(own_weight, move_y(-1)), send(own_weight, move_y(1))
    out_rows = lax.all_gather(out_weight, "seq", axis=0, tiled=True)

    up_rows, down_rows = up_weight.T, down_weight.T
    normed, hidden, slope = call(
        generator_kernel,
        (at, latents[0], gen_gain[None], up_rows),
        [sm, vm, vm, vm],
        [((rows, width), BF16), ((rows, units), BF16), ((rows, units), F32)],
        flops=2 * rows * width * units,
        mib=12,
    )
    own, other = call(
        update_kernel,
        (hidden, down_rows),
        [vm, vm],
        [((4, 16, width), F32), ((4, 16, width), BF16)],
        flops=2 * rows * width * units,
        mib=12,
    )
    (strips,) = call(strips_kernel, (normed,), [vm], [((4, rows, width // 4), BF16)])
    pair = own + send(other, CORE).astype(F32)
    pair, late_hidden, strips, weight_up, weight_down = lax.optimization_barrier(
        (pair, hidden, strips, weight_up, weight_down)
    )
    half = own_weight.shape[0] // 2
    weight_pieces = (
        own_weight,
        weight_up,
        send(weight_down[:half], move_y(1)),
        send(weight_up[half:], move_y(-1)),
        weight_down,
    )
    update = ring_sum(lambda k: pair[k], move_z)
    hidden_line = ring_gather(late_hidden, move_x)
    normed_line = ring_exchange(lambda k: pick(strips, at_y + k), move_y)
    update, weight_pieces, hidden_line, normed_line = lax.optimization_barrier(
        (update, weight_pieces, hidden_line, normed_line)
    )

    quarters, sample_strips = call(
        score_kernel,
        (at, timesteps, update, latents[0], noise_draw[0], score_gain[None]),
        [sm, sm, vm, vm, vm, vm],
        [((4, 16, width // 4), BF16), ((8, 16, share), BF16)],
    )
    crowd = jnp.concatenate(ring_exchange(lambda k: pick(quarters, at_x + k), move_x))
    column, other = group_gather(crowd)
    head_columns = 3 * HEAD + depth
    partials = call(
        project_kernel,
        (at, column.reshape(16 * 16, width // 4), other.reshape(16 * 16, width // 4))
        + weight_pieces,
        [sm] + [hb] * 7,
        [((4 * rows, head_columns), F32)] * 4,
        [
            pltpu.VMEM((4 * rows, width // 4), BF16),
            pltpu.VMEM((width // 4, columns), BF16),
            pltpu.VMEM((4 * rows, columns), F32),
            pltpu.SemaphoreType.DMA((37,)),
        ],
        flops=2 * rows * width * columns,
    )
    near = 2 * rows
    one = send(partials[2][:near].astype(BF16), move_x(1))
    three = send(partials[2][near:].astype(BF16), move_x(-1))
    one = jnp.concatenate([partials[1][:near] + one.astype(F32), partials[1][near:]])
    three = jnp.concatenate([partials[3][:near], partials[3][near:] + three.astype(F32)])
    pair_rows, queries = call(
        finish_kernel,
        [at, partials[0]]
        + [send(one.astype(BF16), to_heads(1)), send(three.astype(BF16), to_heads(3))]
        + [query_up],
        [sm] + [vm] * 4,
        [((4 * rows, 2 * HEAD), BF16), ((8 * rows, HEAD), BF16)],
        flops=8 * rows * depth * HEAD,
    )
    pair_pieces = ring_gather(pair_rows, move_y)

    late_strips, _ = lax.optimization_barrier((sample_strips, pair_rows))
    late_strips = late_strips.reshape(4, 2, 16, share)
    kept = lax.dynamic_index_in_dim(late_strips, at_core, 1, keepdims=False)
    given = lax.dynamic_index_in_dim(late_strips, 1 - at_core, 1, keepdims=False)
    both = jnp.stack([kept, send(given, CORE)], axis=1)
    sample_share = jnp.concatenate(ring_exchange(lambda k: pick(both, at_z + k), move_z))
    sample_share = sample_share.reshape(rows, share)
    pair_pieces, sample_share = lax.optimization_barrier((pair_pieces, sample_share))
    noise_share = relative_rows(
        lax.dynamic_slice_in_dim(noise_draw[0], group * share, share, 1)
    )

    (mixed,) = call(
        attention_kernel,
        [queries] + pair_pieces,
        [vm] + [hb] * 4,
        [((4, 2 * rows, HEAD), BF16)],
        [pltpu.VMEM((16 * rows, 2 * HEAD), BF16), pltpu.SemaphoreType.DMA((4,))],
        flops=64 * rows * rows * 16 * HEAD,
    )
    mixed_pieces = [
        mixed[0],
        send(mixed[3], from_heads(3)),
        send(mixed[2], from_heads(2)),
        send(mixed[1], from_heads(1)),
    ]
    own, other, mixed_fake = call(
        output_kernel,
        [at, out_rows, output_down.T, output_up] + mixed_pieces,
        [sm] + [vm] * 7,
        [
            ((4, 16, width + depth), F32),
            ((4, 16, width + depth), BF16),
            ((rows, head_width), BF16),
        ],
        [pltpu.VMEM((2 * rows, 4 * HEAD), BF16)],
        flops=4 * rows * width * head_width,
    )
    summed = group_sum(own, other)
    column, other = group_gather(
        jnp.concatenate([clip_time * summed[:, :width], summed[:, width:]], axis=1).astype(BF16)
    )
    pre_grad, quarters = call(
        backward_kernel,
        (column, other, down_rows, slope, mixed_fake, sample_share, noise_share),
        [hb] * 2 + [vm] * 5,
        [((rows, units), BF16), ((4, rows + 32, width // 4), BF16)],
        [
            pltpu.VMEM((2, 4, 16, width + depth), BF16),
            pltpu.VMEM((rows, width + depth), BF16),
            pltpu.VMEM((depth, head_width + share + depth), F32),
            pltpu.SemaphoreType.DMA((2,)),
        ],
        flops=2 * rows * width * units,
    )

    def gradient(left, right, position, move):
        part = width // 16
        tall = left[0].shape[0]
        more = 16 if tall > rows else 0
        blocks = call(
            term_kernel,
            (position[None].astype(jnp.int32),) + tuple(left) + tuple(right),
            [sm] + [hb] * 8,
            [((part + more, units), F32)] + [((part + more, units), BF16)] * 3,
            [
                pltpu.VMEM((4, tall, width // 4), BF16),
                pltpu.VMEM((4 * rows, units), BF16),
                pltpu.VMEM((width // 4, units), F32),
                pltpu.SemaphoreType.DMA((8,)),
            ],
            flops=2 * rows * width * units,
        )
        total = ring_sum(lambda k: blocks[k], move)
        half = part // 2
        kept = lax.dynamic_slice_in_dim(total[:part], at_rep * half, half, 0)
        given = lax.dynamic_slice_in_dim(total[:part], (1 - at_rep) * half, half, 0)
        if more:
            kept = jnp.concatenate([kept, total[part:]])
            given = jnp.concatenate([given, total[part:]])
        return kept + send(given.astype(BF16), REP).astype(F32)

    cotangent_line = ring_exchange(lambda k: pick(quarters, at_x + k), move_x)
    down_grad = gradient(cotangent_line, hidden_line, at_y, move_y)
    down_weight_gradient, moments = down_grad[: width // 32], down_grad[width // 32 :]
    pre_line = ring_gather(pre_grad, move_y)
    up_weight_gradient = gradient(normed_line, pre_line, at_x, move_x)

    moments = lax.dynamic_slice_in_dim(moments, at_y * 4 + at_rep * 2, 2, 0)
    through_out = product(split_bf16(moments[:, :head_width]), out_rows, NT)
    through_out = (through_out[:2] + through_out[2:]).reshape(2, 4, 2, share)
    through_out = through_out.transpose(1, 2, 0, 3)
    other = lax.dynamic_index_in_dim(through_out, 1 - at_core, 1, keepdims=False)
    pair = lax.dynamic_index_in_dim(through_out, at_core, 1, keepdims=False)
    pair = pair + send(other.astype(BF16), CORE).astype(F32)
    through_out = ring_sum(lambda k: pick(pair, at_z + k), move_z)
    up_share = lax.dynamic_slice_in_dim(output_up, group * share, share, 1)
    through_up = product(
        split_bf16(moments[:, head_width + share : head_width + share + depth]), up_share, NN
    )
    adapter_up_gradient = (
        through_out
        + moments[:, head_width : head_width + share]
        + through_up[:2]
        + through_up[2:]
    )
    sample_rows = jnp.concatenate(
        [
            lax.dynamic_slice_in_dim(
                sample_share, ((z + 4 - at_z) % 4 * 2 + (c + at_core) % 2) * 16, 16, 0
            )
            for z in range(4)
            for c in range(2)
        ]
    )
    return (sample_rows[None], up_weight_gradient, down_weight_gradient, adapter_up_gradient)


def solution(mesh):
    in_specs = (
        P("rep", "seq", None),
        P("rep", "seq", None),
        P("rep"),
        P(),
        P(None, "grp"),
        P(None, "grp"),
        P(),
        P("seq", None, "grp"),
        P("seq", "grp"),
        P("seq", None),
        P(None, "grp"),
        P("grp", None),
        P(),
    )
    out_specs = (
        P("rep", "seq", "grp"),
        P(("seq", "rep"), "grp"),
        P(("seq", "rep"), "grp"),
        P(("seq", "rep"), "grp"),
    )
    return jax.shard_map(shards, mesh=mesh, in_specs=in_specs, out_specs=out_specs, check_vma=False)
```

```python
import jax
import jax.numpy as jnp
from jax import lax
from jax.experimental import pallas as pl
from jax.experimental.pallas import tpu as pltpu
from jax.sharding import PartitionSpec as P

HEAD = 128
F32 = jnp.float32
BF16 = jnp.bfloat16


def move_x(d):
    return "seq", [(x * 4 + y, ((x + d) % 4) * 4 + y) for x in range(4) for y in range(4)]


def move_y(d):
    return "seq", [(x * 4 + y, x * 4 + (y + d) % 4) for x in range(4) for y in range(4)]


def move_z(d):
    return "grp", [(z * 2 + c, ((z + d) % 4) * 2 + c) for z in range(4) for c in range(2)]


CORE = ("grp", [(z * 2 + c, z * 2 + 1 - c) for z in range(4) for c in range(2)])
REP = ("rep", [(0, 1), (1, 0)])


def send(values, route):
    return lax.ppermute(values, route[0], route[1])


def ring_gather(values, move):
    return [values, send(values, move(-1)), send(values, move(2)), send(values, move(1))]


def ring_gather_parts(values, move):
    up = send(values, move(-1))
    down = send(values, move(1))
    half = values.shape[0] // 2
    first = send(down[:half], move(1))
    second = send(up[half:], move(-1))
    return up, first, second, down


def ring_exchange(block_of, move):
    return [
        block_of(0),
        send(block_of(3), move(3)),
        send(block_of(2), move(2)),
        send(block_of(1), move(1)),
    ]


def ring_sum(block_of, move):
    arrived = [send(block_of(k).astype(BF16), move(k)) for k in (1, 2, 3)]
    total = block_of(0)
    for piece in arrived:
        total = total + piece.astype(F32)
    return total


NN = (((1,), (0,)), ((), ()))
NT = (((1,), (1,)), ((), ()))
TN = (((0,), (0,)), ((), ()))


def product(left, right, dims):
    return lax.dot_general(left, right, dims, preferred_element_type=F32)


def in_vmem():
    return pl.BlockSpec(memory_space=pltpu.VMEM)


def in_smem():
    return pl.BlockSpec(memory_space=pltpu.SMEM)


def anywhere():
    return pl.BlockSpec(memory_space=pl.ANY)


def fetch(sems, *pairs):
    copies = [
        pltpu.make_async_copy(source, target, sems.at[i])
        for i, (source, target) in enumerate(pairs)
    ]
    for copy in copies:
        copy.start()
    return copies


def call(kernel, operands, specs, outs, scratch=(), flops=0, mib=16):
    moved = sum(a.size * a.dtype.itemsize for a in operands)
    return pl.pallas_call(
        kernel,
        out_shape=[jax.ShapeDtypeStruct(shape, kind) for shape, kind in outs],
        in_specs=specs,
        out_specs=[in_vmem() for _ in outs],
        scratch_shapes=list(scratch),
        cost_estimate=pl.CostEstimate(flops=flops, bytes_accessed=moved, transcendentals=0),
        compiler_params=pltpu.CompilerParams(vmem_limit_bytes=mib * 1024 * 1024),
    )(*operands)


def unit_rows(values, gain):
    scale = lax.rsqrt(jnp.mean(values * values, axis=-1, keepdims=True) + 1e-06)
    return values * scale * gain


def pack_kernel(qkv_ref, low_ref, out_ref):
    width = qkv_ref.shape[2]
    for p in range(3):
        out_ref[:, p * width : (p + 1) * width] = qkv_ref[p]
    out_ref[:, 3 * width :] = low_ref[...]


def generator_kernel(at, latent_ref, gain_ref, up_ref, normed_ref, hidden_ref, slope_ref):
    for dz in range(4):
        for dc in range(2):
            block = lax.rem(at[2] + dz, 4) * 2 + lax.rem(at[3] + dc, 2)
            start = pl.multiple_of(block * 16, 16)
            values = latent_ref[pl.ds(start, 16), :].astype(F32)
            first = (dz * 2 + dc) * 16
            normed_ref[first : first + 16, :] = unit_rows(values, gain_ref[...]).astype(BF16)
    pre = product(normed_ref[...], up_ref[...], NT)
    curve = jnp.tanh(0.7978845608028654 * (pre + 0.044715 * (pre * pre * pre)))
    hidden_ref[...] = (0.5 * pre * (1.0 + curve)).astype(BF16)
    slope_ref[...] = 0.5 * (1.0 + curve) + 0.5 * pre * (1.0 - curve * curve) * (
        0.7978845608028654 * (1.0 + 0.134145 * (pre * pre))
    )


def update_kernel(hidden_ref, down_ref, own_ref, other_ref):
    update = product(hidden_ref[...], down_ref[...], NN)
    for dz in range(4):
        own_ref[dz] = update[dz * 32 : dz * 32 + 16]
        other_ref[dz] = update[dz * 32 + 16 : dz * 32 + 32].astype(BF16)


def strips_kernel(normed_ref, out_ref):
    for y in range(4):
        for x in range(4):
            out_ref[y, :, x * 160 : (x + 1) * 160] = normed_ref[
                :, x * 640 + y * 160 : x * 640 + (y + 1) * 160
            ]


def score_kernel(
    at, time, column_ref, other_ref, noise_ref, gain_ref,
    score_ref, sample_ref, noise_out, ordered_ref,
):
    for dz in range(4):
        for dc in range(2):
            block = lax.rem(at[2] + dz, 4) * 2 + lax.rem(at[3] + dc, 2)
            place = pl.ds(pl.multiple_of(block * 16, 16), 16)
            noise = noise_ref[place, :]
            sample = column_ref[dz] if dc == 0 else other_ref[dz]
            cut = slice((dz * 2 + dc) * 16, (dz * 2 + dc) * 16 + 16)
            sample_ref[cut, :] = sample
            ordered_ref[place, :] = sample
            noise_out[cut, :] = noise
            noisy = (1.0 - time[0]) * sample.astype(F32) + time[0] * noise.astype(F32)
            noisy = noisy.astype(BF16).astype(F32)
            score_ref[cut, :] = unit_rows(noisy, gain_ref[...]).astype(BF16)


def project_kernel(score_ref, up_ref, weight_ref, key_ref, value_ref, query_ref):
    result = product(score_ref[...], weight_ref[...], NN)
    width = key_ref.shape[1]
    query = result[:, :width]
    key_ref[...] = result[:, width : 2 * width].astype(BF16)
    value_ref[...] = result[:, 2 * width : 3 * width].astype(BF16)
    low = result[:, 3 * width :].astype(BF16)
    query_ref[:128] = query.astype(BF16)
    query_ref[128:] = (query + product(low, up_ref[...], NN)).astype(BF16)


def attention_kernel(query_ref, *rest):
    pieces, (real_ref, fake_ref, keys, values, sems) = rest[:10], rest[10:]
    width = query_ref.shape[1]
    pairs = []
    for which, target in ((0, keys), (1, values)):
        line, up, opp_a, opp_b, down = pieces[which * 5 : which * 5 + 5]
        for ref, first, count, distance in (
            (line, 0, 4, 0), (up, 0, 4, 1), (opp_a, 0, 2, 2), (opp_b, 2, 2, 2), (down, 0, 4, 3),
        ):
            if which == 0:
                start = (distance * 4 + first) * 128
                pairs.append((ref, target.at[pl.ds(start, count * 128)]))
            else:
                for i in range(count):
                    start = ((first + i) * 4 + distance) * 128
                    pairs.append(
                        (ref.at[pl.ds(i * 128, 128)], target.at[pl.ds(start, 128)])
                    )
    for copy in fetch(sems, *pairs):
        copy.wait()
    for which, mixed_ref in ((0, real_ref), (1, fake_ref)):
        for start in range(0, width, HEAD):
            cut = slice(start, start + HEAD)
            scores = product(
                query_ref[which * 128 : (which + 1) * 128, cut], keys[:, cut], NT
            ) * (HEAD ** (-0.5))
            weights = jnp.exp(scores - jnp.max(scores, axis=-1, keepdims=True))
            total = jnp.sum(weights, axis=-1, keepdims=True)
            mix = product(weights.astype(BF16), values[:, cut], NN) / total
            mixed_ref[:, cut] = mix.astype(BF16)


def output_kernel(real_ref, fake_ref, out_ref, down_ref, up_ref, own_ref, other_ref):
    real, fake = real_ref[...], fake_ref[...]
    latent = product(fake, down_ref[...], NT)
    high = latent.astype(BF16)
    low = (latent - high.astype(F32)).astype(BF16)
    difference = (
        product(real, out_ref[...], NT)
        - product(fake, out_ref[...], NT)
        - (product(high, up_ref[...], NN) + product(low, up_ref[...], NN))
    )
    features = out_ref.shape[0]
    for dz in range(4):
        cut = slice(dz * 32, dz * 32 + 16)
        own_ref[dz, :, :features] = difference[cut]
        own_ref[dz, :, features:] = latent[cut]
        cut = slice(dz * 32 + 16, dz * 32 + 32)
        other_ref[dz, :, :features] = difference[cut].astype(BF16)
        other_ref[dz, :, features:] = latent[cut].astype(BF16)


def backward_kernel(
    column_hbm, other_hbm, down_ref, slope_ref, fake_ref, sample_ref, noise_ref,
    pre_ref, quarters_ref, both, whole, wide, sems,
):
    for copy in fetch(sems, (column_hbm, both.at[0]), (other_hbm, both.at[1])):
        copy.wait()
    features = down_ref.shape[1]
    quarter = features // 4
    for dz in range(4):
        for dc in range(2):
            cut = slice((dz * 2 + dc) * 16, (dz * 2 + dc) * 16 + 16)
            whole[cut, :] = both[dc, dz]
    for x in range(4):
        quarters_ref[x, :128, :] = whole[:, x * quarter : (x + 1) * quarter]
    latent = whole[:, features:]
    width, share, depth = fake_ref.shape[1], sample_ref.shape[1], latent.shape[1]
    error = sample_ref[...].astype(F32) - noise_ref[...].astype(F32)
    high = error.astype(BF16)
    wide[:, :width] = product(latent, fake_ref[...], TN)
    wide[:, width : width + share] = product(latent, high, TN) + product(
        latent, (error - high.astype(F32)).astype(BF16), TN
    )
    wide[:, width + share :] = product(latent, latent, TN)
    for x in range(4):
        quarters_ref[x, 128:144, :] = wide[x * 16 : x * 16 + 16, :quarter].astype(BF16)
        quarters_ref[x, 144:160, :] = jnp.zeros((16, quarter), BF16)
        quarters_ref[x, 144:160, : width + share + depth - quarter] = wide[
            x * 16 : x * 16 + 16, quarter:
        ].astype(BF16)
    grad = product(whole[:, :features], down_ref[...], NT)
    pre_ref[...] = (grad * slope_ref[...]).astype(BF16)


def join_kernel(*refs):
    for ref, first in ((refs[8], 0), (refs[9], 4)):
        rows = refs[first].shape[0]
        for i in range(4):
            ref[i * rows : (i + 1) * rows, :] = refs[first + i][...]


def term_kernel(at, hidden_ref, normed_ref, *rest):
    cotangents, pres = rest[:4], rest[4:8]
    down_outs, up_outs, (extra_ref, term) = rest[8:12], rest[12:16], rest[16:]
    rows = jnp.concatenate([ref[:128, :] for ref in cotangents])
    term[...] = product(rows, hidden_ref[...], TN)
    for k in range(4):
        start = pl.multiple_of(lax.rem(at[1] + k, 4) * 160, 16)
        down_outs[k][...] = term[pl.ds(start, 160), :].astype(down_outs[k].dtype)
    term[...] = product(normed_ref[...], jnp.concatenate([ref[...] for ref in pres]), TN)
    for k in range(4):
        start = pl.multiple_of(lax.rem(at[0] + k, 4) * 160, 16)
        up_outs[k][...] = term[pl.ds(start, 160), :].astype(up_outs[k].dtype)
    extra = cotangents[0][128:, :].astype(F32)
    for ref in cotangents[1:]:
        extra = extra + ref[128:, :].astype(F32)
    extra_ref[:, :640] = extra[:16]
    extra_ref[:, 640:] = extra[16:, :128]


def moments_kernel(moments_ref, out_ref, strips_ref):
    width = out_ref.shape[1]
    rows = moments_ref[:, :width]
    high = rows.astype(BF16)
    low = (rows - high.astype(F32)).astype(BF16)
    through = product(high, out_ref[...], NT) + product(low, out_ref[...], NT)
    for g in range(8):
        strips_ref[g] = through[:, g * 320 : (g + 1) * 320]


def group_sum(own, other):
    pair = own + send(other, CORE).astype(F32)
    return ring_sum(lambda k: pair[k], move_z)


def group_gather(rows):
    column = jnp.stack(ring_gather(rows, move_z))
    return column, send(column, CORE)


def spread(values, first_move, second_move):
    up, opp_a, opp_b, down = ring_gather_parts(values, first_move)
    line = jnp.concatenate([values, up, opp_a, opp_b, down])
    return (line,) + ring_gather_parts(line, second_move)


def split_bf16(values):
    high = values.astype(BF16)
    return jnp.concatenate([high, (values - high.astype(F32)).astype(BF16)])


def shards(
    latents,
    noise_draw,
    timesteps,
    gen_gain,
    up_weight,
    down_weight,
    score_gain,
    qkv_weight,
    out_weight,
    query_down,
    query_up,
    output_down,
    output_up,
):
    place = lax.axis_index("seq")
    at_x, at_y = place // 4, place % 4
    group = lax.axis_index("grp")
    at_z, at_core = group // 2, group % 2
    at_rep = lax.axis_index("rep")
    at = jnp.stack([at_x, at_y, at_z, at_core]).astype(jnp.int32)
    clip_time = timesteps[0]
    rows, width = latents.shape[1:]
    units = up_weight.shape[1]
    share = width // 8
    head_width = out_weight.shape[1]
    depth = query_down.shape[1]
    vm, sm, hb = in_vmem(), in_smem(), anywhere()


    def pick(values, index):
        return lax.dynamic_index_in_dim(values, index % 4, 0, keepdims=False)

    vector_rows = qkv_weight.shape[0]
    (own_weight,) = call(
        pack_kernel,
        (qkv_weight.transpose(1, 0, 2), query_down),
        [vm, vm],
        [((vector_rows, 3 * head_width + depth), BF16)],
        mib=8,
    )
    score_weight = lax.all_gather(own_weight, "seq", axis=0, tiled=True)
    columns = score_weight.shape[1]

    up_rows, down_rows = up_weight.T, down_weight.T
    normed, hidden, slope = call(
        generator_kernel,
        (at, latents[0], gen_gain[None], up_rows),
        [sm, vm, vm, vm],
        [((rows, width), BF16), ((rows, units), BF16), ((rows, units), F32)],
        flops=2 * rows * width * units,
        mib=12,
    )
    own, other = call(
        update_kernel,
        (hidden, down_rows),
        [vm, vm],
        [((4, 16, width), F32), ((4, 16, width), BF16)],
        flops=2 * rows * width * units,
        mib=12,
    )
    (strips,) = call(strips_kernel, (normed,), [vm], [((4, rows, width // 4), BF16)])
    update = group_sum(own, other)
    latent_own = lax.dynamic_slice_in_dim(latents[0], group * 16, 16, 0)
    column, other = group_gather((latent_own.astype(F32) + update).astype(BF16))

    score_in, sample, noise_rows, ordered = call(
        score_kernel,
        (at, timesteps, column, other, noise_draw[0], score_gain[None]),
        [sm, sm, vm, vm, vm, vm],
        [((rows, width), BF16)] * 4,
    )
    sample_out = lax.dynamic_slice_in_dim(ordered, group * share, share, 1)
    sample_share = lax.dynamic_slice_in_dim(sample, group * share, share, 1)
    noise_share = lax.dynamic_slice_in_dim(noise_rows, group * share, share, 1)

    late_hidden, strips, score_in, late_out, sample_out = lax.optimization_barrier(
        (hidden, strips, score_in, out_weight, sample_out)
    )
    out_rows = lax.all_gather(late_out, "seq", axis=0, tiled=True)
    hidden_line = ring_gather(late_hidden, move_x)
    normed_line = ring_exchange(lambda k: pick(strips, at_y + k), move_y)
    hidden_line, normed_line = call(
        join_kernel,
        tuple(hidden_line) + tuple(normed_line),
        [vm] * 8,
        [((4 * rows, units), BF16), ((4 * rows, width // 4), BF16)],
        mib=8,
    )
    score_in, hidden_line, normed_line, sample_out, sample_share, noise_share = (
        lax.optimization_barrier(
            (score_in, hidden_line, normed_line, sample_out, sample_share, noise_share)
        )
    )
    key_rows, value_rows, queries = call(
        project_kernel,
        (score_in, query_up, score_weight),
        [vm, vm, vm],
        [((rows, head_width), BF16), ((rows, head_width), BF16), ((2 * rows, head_width), BF16)],
        flops=2 * rows * width * columns,
    )

    key_pieces = spread(key_rows, move_x, move_y)
    value_pieces = spread(value_rows, move_y, move_x)
    mixed_real, mixed_fake = call(
        attention_kernel,
        (queries,) + key_pieces + value_pieces,
        [vm] + [hb] * 10,
        [((rows, head_width), BF16)] * 2,
        [pltpu.VMEM((16 * rows, head_width), BF16)] * 2 + [pltpu.SemaphoreType.DMA((21,))],
        flops=16 * rows * rows * 16 * head_width,
    )
    own, other = call(
        output_kernel,
        (mixed_real, mixed_fake, out_rows, output_down.T, output_up),
        [vm] * 5,
        [((4, 16, width + depth), F32), ((4, 16, width + depth), BF16)],
        flops=4 * rows * width * head_width,
    )
    summed = group_sum(own, other)
    column, other = group_gather(
        jnp.concatenate([clip_time * summed[:, :width], summed[:, width:]], axis=1).astype(BF16)
    )
    pre_grad, quarters = call(
        backward_kernel,
        (column, other, down_rows, slope, mixed_fake, sample_share, noise_share),
        [hb] * 2 + [vm] * 5,
        [((rows, units), BF16), ((4, rows + 32, width // 4), BF16)],
        [
            pltpu.VMEM((2, 4, 16, width + depth), BF16),
            pltpu.VMEM((rows, width + depth), BF16),
            pltpu.VMEM((depth, head_width + share + depth), F32),
            pltpu.SemaphoreType.DMA((2,)),
        ],
        flops=2 * rows * width * units,
    )

    part = width // 16

    def rep_sum(total, more=None):
        half = part // 2
        kept = lax.dynamic_slice_in_dim(total, at_rep * half, half, 0)
        given = lax.dynamic_slice_in_dim(total, (1 - at_rep) * half, half, 0)
        if more is not None:
            more = jnp.pad(more, ((0, 16 - more.shape[0]), (0, units - more.shape[1])))
            kept, given = jnp.concatenate([kept, more]), jnp.concatenate([given, more])
        return kept + send(given.astype(BF16), REP).astype(F32)

    cotangent_line = ring_exchange(lambda k: pick(quarters, at_x + k), move_x)
    pre_line = ring_gather(pre_grad, move_y)
    blocks = call(
        term_kernel,
        (at, hidden_line, normed_line) + tuple(cotangent_line) + tuple(pre_line),
        [sm] + [vm] * 10,
        ([((part, units), F32)] + [((part, units), BF16)] * 3) * 2
        + [((16, head_width + share + depth), F32)],
        [pltpu.VMEM((width // 4, units), F32)],
        flops=4 * rows * width * units,
        mib=20,
    )
    down_arrived = [send(blocks[k], move_y(k)) for k in (1, 2, 3)]
    up_arrived = [send(blocks[4 + k], move_x(k)) for k in (1, 2, 3)]
    moments, down_arrived[0], up_arrived[0] = lax.optimization_barrier(
        (blocks[8], down_arrived[0], up_arrived[0])
    )
    down_total, up_total = blocks[0], blocks[4]
    for k in range(3):
        down_total = down_total + down_arrived[k].astype(F32)
        up_total = up_total + up_arrived[k].astype(F32)

    (out_strips,) = call(
        moments_kernel,
        (moments, out_rows),
        [vm, vm],
        [((8, 16, share), F32)],
        flops=64 * width * head_width,
    )
    out_strips = out_strips.reshape(4, 2, 16, share)
    other = lax.dynamic_index_in_dim(out_strips, 1 - at_core, 1, keepdims=False)
    pair = lax.dynamic_index_in_dim(out_strips, at_core, 1, keepdims=False)
    pair = pair + send(other.astype(BF16), CORE).astype(F32)
    through_out = ring_sum(lambda k: pick(pair, at_z + k), move_z)
    up_share = lax.dynamic_slice_in_dim(output_up, group * share, share, 1)
    through_up = product(split_bf16(moments[:, head_width + share :]), up_share, NN)
    adapter = (
        through_out
        + moments[:, head_width : head_width + share]
        + through_up[:16]
        + through_up[16:]
    ).reshape(4, 4, share)
    adapter = ring_sum(lambda k: pick(adapter, at_y + k), move_y)

    down_weight_gradient = rep_sum(down_total)
    up_weight_gradient = rep_sum(up_total, adapter)
    adapter_up_gradient = lax.dynamic_slice(
        up_weight_gradient, (part // 2 + at_rep * 2, 0), (2, share)
    )
    up_weight_gradient = up_weight_gradient[: part // 2]
    return (sample_out[None], up_weight_gradient, down_weight_gradient, adapter_up_gradient)


def solution(mesh):
    in_specs = (
        P("rep", "seq", None),
        P("rep", "seq", None),
        P("rep"),
        P(),
        P(None, "grp"),
        P(None, "grp"),
        P(),
        P("seq", None, "grp"),
        P("seq", "grp"),
        P("seq", None),
        P(None, "grp"),
        P("grp", None),
        P(),
    )
    out_specs = (
        P("rep", "seq", "grp"),
        P(("seq", "rep"), "grp"),
        P(("seq", "rep"), "grp"),
        P(("seq", "rep"), "grp"),
    )
    return jax.shard_map(shards, mesh=mesh, in_specs=in_specs, out_specs=out_specs, check_vma=False)
```

```python
import jax
import jax.numpy as jnp
from jax import lax
from jax.experimental import pallas as pl
from jax.experimental.pallas import tpu as pltpu
from jax.sharding import PartitionSpec as P

HEAD = 128
F32 = jnp.float32
BF16 = jnp.bfloat16


def move_x(d):
    return "seq", [(x * 4 + y, ((x + d) % 4) * 4 + y) for x in range(4) for y in range(4)]


def move_y(d):
    return "seq", [(x * 4 + y, x * 4 + (y + d) % 4) for x in range(4) for y in range(4)]


def move_z(d):
    return "grp", [(z * 2 + c, ((z + d) % 4) * 2 + c) for z in range(4) for c in range(2)]


CORE = ("grp", [(z * 2 + c, z * 2 + 1 - c) for z in range(4) for c in range(2)])
REP = ("rep", [(0, 1), (1, 0)])


def send(values, route):
    return lax.ppermute(values, route[0], route[1])


def ring_gather(values, move):
    return [values, send(values, move(-1)), send(values, move(2)), send(values, move(1))]


def ring_gather_parts(values, move):
    up = send(values, move(-1))
    down = send(values, move(1))
    half = values.shape[0] // 2
    first = send(down[:half], move(1))
    second = send(up[half:], move(-1))
    return up, first, second, down


def ring_exchange(block_of, move):
    return [
        block_of(0),
        send(block_of(3), move(3)),
        send(block_of(2), move(2)),
        send(block_of(1), move(1)),
    ]


def ring_sum(block_of, move):
    arrived = [send(block_of(k).astype(BF16), move(k)) for k in (1, 2, 3)]
    total = block_of(0)
    for piece in arrived:
        total = total + piece.astype(F32)
    return total


NN = (((1,), (0,)), ((), ()))
NT = (((1,), (1,)), ((), ()))
TN = (((0,), (0,)), ((), ()))


def product(left, right, dims):
    return lax.dot_general(left, right, dims, preferred_element_type=F32)


def in_vmem():
    return pl.BlockSpec(memory_space=pltpu.VMEM)


def in_smem():
    return pl.BlockSpec(memory_space=pltpu.SMEM)


def anywhere():
    return pl.BlockSpec(memory_space=pl.ANY)


def fetch(sems, *pairs):
    copies = [
        pltpu.make_async_copy(source, target, sems.at[i])
        for i, (source, target) in enumerate(pairs)
    ]
    for copy in copies:
        copy.start()
    return copies


def call(kernel, operands, specs, outs, scratch=(), flops=0, mib=16):
    moved = sum(a.size * a.dtype.itemsize for a in operands)
    return pl.pallas_call(
        kernel,
        out_shape=[jax.ShapeDtypeStruct(shape, kind) for shape, kind in outs],
        in_specs=specs,
        out_specs=[in_vmem() for _ in outs],
        scratch_shapes=list(scratch),
        cost_estimate=pl.CostEstimate(flops=flops, bytes_accessed=moved, transcendentals=0),
        compiler_params=pltpu.CompilerParams(vmem_limit_bytes=mib * 1024 * 1024),
    )(*operands)


def unit_rows(values, gain):
    scale = lax.rsqrt(jnp.mean(values * values, axis=-1, keepdims=True) + 1e-06)
    return values * scale * gain


def pack_kernel(qkv_ref, low_ref, out_ref):
    width = qkv_ref.shape[2]
    for p in range(3):
        out_ref[:, p * width : (p + 1) * width] = qkv_ref[p]
    out_ref[:, 3 * width :] = low_ref[...]


def generator_kernel(at, latent_ref, gain_ref, up_ref, normed_ref, hidden_ref, slope_ref):
    for dz in range(4):
        for dc in range(2):
            block = lax.rem(at[2] + dz, 4) * 2 + lax.rem(at[3] + dc, 2)
            start = pl.multiple_of(block * 16, 16)
            values = latent_ref[pl.ds(start, 16), :].astype(F32)
            first = (dz * 2 + dc) * 16
            normed_ref[first : first + 16, :] = unit_rows(values, gain_ref[...]).astype(BF16)
    pre = product(normed_ref[...], up_ref[...], NT)
    curve = jnp.tanh(0.7978845608028654 * (pre + 0.044715 * (pre * pre * pre)))
    hidden_ref[...] = (0.5 * pre * (1.0 + curve)).astype(BF16)
    slope_ref[...] = 0.5 * (1.0 + curve) + 0.5 * pre * (1.0 - curve * curve) * (
        0.7978845608028654 * (1.0 + 0.134145 * (pre * pre))
    )


def update_kernel(hidden_ref, down_ref, own_ref, other_ref):
    update = product(hidden_ref[...], down_ref[...], NN)
    for dz in range(4):
        own_ref[dz] = update[dz * 32 : dz * 32 + 16]
        other_ref[dz] = update[dz * 32 + 16 : dz * 32 + 32].astype(BF16)


def strips_kernel(normed_ref, out_ref):
    for y in range(4):
        for x in range(4):
            out_ref[y, :, x * 160 : (x + 1) * 160] = normed_ref[
                :, x * 640 + y * 160 : x * 640 + (y + 1) * 160
            ]


def score_kernel(
    at, time, column_ref, other_ref, noise_ref, gain_ref,
    score_ref, sample_ref, noise_out, ordered_ref,
):
    for dz in range(4):
        for dc in range(2):
            block = lax.rem(at[2] + dz, 4) * 2 + lax.rem(at[3] + dc, 2)
            place = pl.ds(pl.multiple_of(block * 16, 16), 16)
            noise = noise_ref[place, :]
            sample = column_ref[dz] if dc == 0 else other_ref[dz]
            cut = slice((dz * 2 + dc) * 16, (dz * 2 + dc) * 16 + 16)
            sample_ref[cut, :] = sample
            ordered_ref[place, :] = sample
            noise_out[cut, :] = noise
            noisy = (1.0 - time[0]) * sample.astype(F32) + time[0] * noise.astype(F32)
            noisy = noisy.astype(BF16).astype(F32)
            score_ref[cut, :] = unit_rows(noisy, gain_ref[...]).astype(BF16)


def project_kernel(score_ref, up_ref, weight_ref, key_ref, value_ref, query_ref):
    result = product(score_ref[...], weight_ref[...], NN)
    width = key_ref.shape[1]
    query = result[:, :width]
    key_ref[...] = result[:, width : 2 * width].astype(BF16)
    value_ref[...] = result[:, 2 * width : 3 * width].astype(BF16)
    low = result[:, 3 * width :].astype(BF16)
    query_ref[:128] = query.astype(BF16)
    query_ref[128:] = (query + product(low, up_ref[...], NN)).astype(BF16)


def attention_kernel(query_ref, *rest):
    pieces, (real_ref, fake_ref, keys, values, sems) = rest[:10], rest[10:]
    width = query_ref.shape[1]
    pairs = []
    for which, target in ((0, keys), (1, values)):
        line, up, opp_a, opp_b, down = pieces[which * 5 : which * 5 + 5]
        for ref, first, count, distance in (
            (line, 0, 4, 0), (up, 0, 4, 1), (opp_a, 0, 2, 2), (opp_b, 2, 2, 2), (down, 0, 4, 3),
        ):
            if which == 0:
                start = (distance * 4 + first) * 128
                pairs.append((ref, target.at[pl.ds(start, count * 128)]))
            else:
                for i in range(count):
                    start = ((first + i) * 4 + distance) * 128
                    pairs.append(
                        (ref.at[pl.ds(i * 128, 128)], target.at[pl.ds(start, 128)])
                    )
    for copy in fetch(sems, *pairs):
        copy.wait()
    for which, mixed_ref in ((0, real_ref), (1, fake_ref)):
        for start in range(0, width, HEAD):
            cut = slice(start, start + HEAD)
            scores = product(
                query_ref[which * 128 : (which + 1) * 128, cut], keys[:, cut], NT
            ) * (HEAD ** (-0.5))
            weights = jnp.exp(scores - jnp.max(scores, axis=-1, keepdims=True))
            total = jnp.sum(weights, axis=-1, keepdims=True)
            mix = product(weights.astype(BF16), values[:, cut], NN) / total
            mixed_ref[:, cut] = mix.astype(BF16)


def output_kernel(real_ref, fake_ref, out_ref, down_ref, up_ref, own_ref, other_ref):
    real, fake = real_ref[...], fake_ref[...]
    out = out_ref[...]
    latent = product(fake, down_ref[...], NT)
    high = latent.astype(BF16)
    low = (latent - high.astype(F32)).astype(BF16)
    difference = (
        product(real, out, NT)
        - product(fake, out, NT)
        - (product(high, up_ref[...], NN) + product(low, up_ref[...], NN))
    )
    features = out_ref.shape[0]
    for dz in range(4):
        cut = slice(dz * 32, dz * 32 + 16)
        own_ref[dz, :, :features] = difference[cut]
        own_ref[dz, :, features:] = latent[cut]
        cut = slice(dz * 32 + 16, dz * 32 + 32)
        other_ref[dz, :, :features] = difference[cut].astype(BF16)
        other_ref[dz, :, features:] = latent[cut].astype(BF16)


def backward_kernel(
    column_hbm, other_hbm, down_ref, slope_ref, fake_ref, sample_ref, noise_ref,
    pre_ref, quarters_ref, both, whole, wide, sems,
):
    for copy in fetch(sems, (column_hbm, both.at[0]), (other_hbm, both.at[1])):
        copy.wait()
    features = down_ref.shape[1]
    quarter = features // 4
    for dz in range(4):
        for dc in range(2):
            cut = slice((dz * 2 + dc) * 16, (dz * 2 + dc) * 16 + 16)
            whole[cut, :] = both[dc, dz]
    for x in range(4):
        quarters_ref[x, :128, :] = whole[:, x * quarter : (x + 1) * quarter]
    latent = whole[:, features:]
    width, share, depth = fake_ref.shape[1], sample_ref.shape[1], latent.shape[1]
    error = sample_ref[...].astype(F32) - noise_ref[...].astype(F32)
    high = error.astype(BF16)
    wide[:, :width] = product(latent, fake_ref[...], TN)
    wide[:, width : width + share] = product(latent, high, TN) + product(
        latent, (error - high.astype(F32)).astype(BF16), TN
    )
    wide[:, width + share :] = product(latent, latent, TN)
    for x in range(4):
        quarters_ref[x, 128:144, :] = wide[x * 16 : x * 16 + 16, :quarter].astype(BF16)
        quarters_ref[x, 144:160, :] = jnp.zeros((16, quarter), BF16)
        quarters_ref[x, 144:160, : width + share + depth - quarter] = wide[
            x * 16 : x * 16 + 16, quarter:
        ].astype(BF16)
    grad = product(whole[:, :features], down_ref[...], NT)
    pre_ref[...] = (grad * slope_ref[...]).astype(BF16)


def join_kernel(*refs):
    for ref, first in ((refs[8], 0), (refs[9], 4)):
        rows = refs[first].shape[0]
        for i in range(4):
            ref[i * rows : (i + 1) * rows, :] = refs[first + i][...]


def term_kernel(at, hidden_ref, normed_ref, *rest):
    cotangents, pres = rest[:4], rest[4:8]
    down_outs, up_outs, (term,) = rest[8:12], rest[12:16], rest[16:]
    rows = jnp.concatenate([ref[:128, :] for ref in cotangents])
    term[...] = product(rows, hidden_ref[...], TN)
    for k in range(4):
        start = pl.multiple_of(lax.rem(at[1] + k, 4) * 160, 16)
        down_outs[k][:160, :] = term[pl.ds(start, 160), :].astype(down_outs[k].dtype)
    term[...] = product(normed_ref[...], jnp.concatenate([ref[...] for ref in pres]), TN)
    for k in range(4):
        start = pl.multiple_of(lax.rem(at[0] + k, 4) * 160, 16)
        up_outs[k][...] = term[pl.ds(start, 160), :].astype(up_outs[k].dtype)
    extra = cotangents[0][128:, :].astype(F32)
    for ref in cotangents[1:]:
        extra = extra + ref[128:, :].astype(F32)
    for ref in down_outs:
        ref[160:, :] = jnp.zeros((16, ref.shape[1]), ref.dtype)
        ref[160:, :640] = extra[:16].astype(ref.dtype)
        ref[160:, 640:768] = extra[16:, :128].astype(ref.dtype)


def moments_kernel(moments_ref, out_ref, strips_ref):
    width = 3 * HEAD
    out = out_ref[...]
    rows = moments_ref[:, :width]
    high = rows.astype(BF16)
    low = (rows - high.astype(F32)).astype(BF16)
    through = product(high, out, NT) + product(low, out, NT)
    for g in range(8):
        strips_ref[g] = through[:, g * 320 : (g + 1) * 320]


def group_sum(own, other):
    pair = own + send(other, CORE).astype(F32)
    return ring_sum(lambda k: pair[k], move_z)


def group_gather(rows):
    column = jnp.stack(ring_gather(rows, move_z))
    return column, send(column, CORE)


def spread(values, first_move, second_move):
    up, opp_a, opp_b, down = ring_gather_parts(values, first_move)
    line = jnp.concatenate([values, up, opp_a, opp_b, down])
    return (line,) + ring_gather_parts(line, second_move)


def split_bf16(values):
    high = values.astype(BF16)
    return jnp.concatenate([high, (values - high.astype(F32)).astype(BF16)])


def shards(
    latents,
    noise_draw,
    timesteps,
    gen_gain,
    up_weight,
    down_weight,
    score_gain,
    qkv_weight,
    out_weight,
    query_down,
    query_up,
    output_down,
    output_up,
):
    place = lax.axis_index("seq")
    at_x, at_y = place // 4, place % 4
    group = lax.axis_index("grp")
    at_z, at_core = group // 2, group % 2
    at_rep = lax.axis_index("rep")
    at = jnp.stack([at_x, at_y, at_z, at_core]).astype(jnp.int32)
    clip_time = timesteps[0]
    rows, width = latents.shape[1:]
    units = up_weight.shape[1]
    share = width // 8
    head_width = out_weight.shape[1]
    depth = query_down.shape[1]
    vm, sm, hb = in_vmem(), in_smem(), anywhere()


    def pick(values, index):
        return lax.dynamic_index_in_dim(values, index % 4, 0, keepdims=False)

    vector_rows = qkv_weight.shape[0]
    (own_weight,) = call(
        pack_kernel,
        (qkv_weight.transpose(1, 0, 2), query_down),
        [vm, vm],
        [((vector_rows, 3 * head_width + depth), BF16)],
        mib=8,
    )
    score_weight = lax.all_gather(own_weight, "seq", axis=0, tiled=True)
    columns = score_weight.shape[1]

    up_rows, down_rows = up_weight.T, down_weight.T
    normed, hidden, slope = call(
        generator_kernel,
        (at, latents[0], gen_gain[None], up_rows),
        [sm, vm, vm, vm],
        [((rows, width), BF16), ((rows, units), BF16), ((rows, units), F32)],
        flops=2 * rows * width * units,
        mib=12,
    )
    own, other = call(
        update_kernel,
        (hidden, down_rows),
        [vm, vm],
        [((4, 16, width), F32), ((4, 16, width), BF16)],
        flops=2 * rows * width * units,
        mib=12,
    )
    (strips,) = call(strips_kernel, (normed,), [vm], [((4, rows, width // 4), BF16)])
    update = group_sum(own, other)
    update, late_hidden, strips, late_out = lax.optimization_barrier(
        (update, hidden, strips, out_weight)
    )
    out_rows = lax.all_gather(late_out, "seq", axis=0, tiled=True)
    hidden_line = ring_gather(late_hidden, move_x)
    normed_line = ring_exchange(lambda k: pick(strips, at_y + k), move_y)
    latent_own = lax.dynamic_slice_in_dim(latents[0], group * 16, 16, 0)
    column, other = group_gather((latent_own.astype(F32) + update).astype(BF16))

    score_in, sample, noise_rows, ordered = call(
        score_kernel,
        (at, timesteps, column, other, noise_draw[0], score_gain[None]),
        [sm, sm, vm, vm, vm, vm],
        [((rows, width), BF16)] * 4,
    )
    sample_out = lax.dynamic_slice_in_dim(ordered, group * share, share, 1)
    sample_share = lax.dynamic_slice_in_dim(sample, group * share, share, 1)
    noise_share = lax.dynamic_slice_in_dim(noise_rows, group * share, share, 1)

    hidden_line, normed_line = call(
        join_kernel,
        tuple(hidden_line) + tuple(normed_line),
        [vm] * 8,
        [((4 * rows, units), BF16), ((4 * rows, width // 4), BF16)],
        mib=8,
    )
    score_in, hidden_line, normed_line, sample_out, sample_share, noise_share = (
        lax.optimization_barrier(
            (score_in, hidden_line, normed_line, sample_out, sample_share, noise_share)
        )
    )
    key_rows, value_rows, queries = call(
        project_kernel,
        (score_in, query_up, score_weight),
        [vm, vm, vm],
        [((rows, head_width), BF16), ((rows, head_width), BF16), ((2 * rows, head_width), BF16)],
        flops=2 * rows * width * columns,
    )

    key_pieces = spread(key_rows, move_x, move_y)
    value_pieces = spread(value_rows, move_y, move_x)
    mixed_real, mixed_fake = call(
        attention_kernel,
        (queries,) + key_pieces + value_pieces,
        [vm] + [hb] * 10,
        [((rows, head_width), BF16)] * 2,
        [pltpu.VMEM((16 * rows, head_width), BF16)] * 2 + [pltpu.SemaphoreType.DMA((21,))],
        flops=16 * rows * rows * 16 * head_width,
    )
    own, other = call(
        output_kernel,
        (mixed_real, mixed_fake, out_rows, output_down.T, output_up),
        [vm] * 5,
        [((4, 16, width + depth), F32), ((4, 16, width + depth), BF16)],
        flops=4 * rows * width * head_width,
    )
    summed = group_sum(own, other)
    column, other = group_gather(
        jnp.concatenate([clip_time * summed[:, :width], summed[:, width:]], axis=1).astype(BF16)
    )
    pre_grad, quarters = call(
        backward_kernel,
        (column, other, down_rows, slope, mixed_fake, sample_share, noise_share),
        [hb] * 2 + [vm] * 5,
        [((rows, units), BF16), ((4, rows + 32, width // 4), BF16)],
        [
            pltpu.VMEM((2, 4, 16, width + depth), BF16),
            pltpu.VMEM((rows, width + depth), BF16),
            pltpu.VMEM((depth, head_width + share + depth), F32),
            pltpu.SemaphoreType.DMA((2,)),
        ],
        flops=2 * rows * width * units,
    )

    part = width // 16

    def rep_sum(total):
        half = total.shape[0] // 2
        kept = lax.dynamic_slice_in_dim(total, at_rep * half, half, 0)
        given = lax.dynamic_slice_in_dim(total, (1 - at_rep) * half, half, 0)
        return kept + send(given.astype(BF16), REP).astype(F32)

    cotangent_line = ring_exchange(lambda k: pick(quarters, at_x + k), move_x)
    pre_line = ring_gather(pre_grad, move_y)
    blocks = call(
        term_kernel,
        (at, hidden_line, normed_line) + tuple(cotangent_line) + tuple(pre_line),
        [sm] + [vm] * 10,
        [((part + 16, units), F32)]
        + [((part + 16, units), BF16)] * 3
        + [((part, units), F32)]
        + [((part, units), BF16)] * 3,
        [pltpu.VMEM((width // 4, units), F32)],
        flops=4 * rows * width * units,
        mib=20,
    )
    down_arrived = [send(blocks[k], move_y(k)) for k in (1, 2, 3)]
    up_arrived = [send(blocks[4 + k], move_x(k)) for k in (1, 2, 3)]
    down_total, up_total = blocks[0], blocks[4]
    for k in range(3):
        down_total = down_total + down_arrived[k].astype(F32)
        up_total = up_total + up_arrived[k].astype(F32)

    down_weight_gradient = rep_sum(down_total[:part])
    up_weight_gradient = rep_sum(up_total)

    moments = down_total[part:, : head_width + share + depth]
    (out_strips,) = call(
        moments_kernel,
        (moments, out_rows),
        [vm, vm],
        [((8, 16, share), F32)],
        flops=64 * width * head_width,
    )
    moments = lax.dynamic_slice_in_dim(moments, at_y * 4, 4, 0)
    out_strips = lax.dynamic_slice_in_dim(out_strips, at_y * 4, 4, 1).reshape(4, 2, 4, share)
    other = lax.dynamic_index_in_dim(out_strips, 1 - at_core, 1, keepdims=False)
    pair = lax.dynamic_index_in_dim(out_strips, at_core, 1, keepdims=False)
    pair = pair + send(other.astype(BF16), CORE).astype(F32)
    through_out = ring_sum(lambda k: pick(pair, at_z + k), move_z)
    up_share = lax.dynamic_slice_in_dim(output_up, group * share, share, 1)
    through_up = product(split_bf16(moments[:, head_width + share :]), up_share, NN)
    adapter_up_gradient = rep_sum(
        through_out
        + moments[:, head_width : head_width + share]
        + through_up[:4]
        + through_up[4:]
    )
    return (sample_out[None], up_weight_gradient, down_weight_gradient, adapter_up_gradient)


def solution(mesh):
    in_specs = (
        P("rep", "seq", None),
        P("rep", "seq", None),
        P("rep"),
        P(),
        P(None, "grp"),
        P(None, "grp"),
        P(),
        P("seq", None, "grp"),
        P("seq", "grp"),
        P("seq", None),
        P(None, "grp"),
        P("grp", None),
        P(),
    )
    out_specs = (
        P("rep", "seq", "grp"),
        P(("seq", "rep"), "grp"),
        P(("seq", "rep"), "grp"),
        P(("seq", "rep"), "grp"),
    )
    return jax.shard_map(shards, mesh=mesh, in_specs=in_specs, out_specs=out_specs, check_vma=False)
```

```python
import jax
import jax.numpy as jnp
from jax import lax
from jax.experimental import pallas as pl
from jax.experimental.pallas import tpu as pltpu
from jax.sharding import PartitionSpec as P

HEAD = 128
F32 = jnp.float32
BF16 = jnp.bfloat16


def move_x(d):
    return "seq", [(x * 4 + y, ((x + d) % 4) * 4 + y) for x in range(4) for y in range(4)]


def move_y(d):
    return "seq", [(x * 4 + y, x * 4 + (y + d) % 4) for x in range(4) for y in range(4)]


def move_z(d):
    return "grp", [(z * 2 + c, ((z + d) % 4) * 2 + c) for z in range(4) for c in range(2)]


CORE = ("grp", [(z * 2 + c, z * 2 + 1 - c) for z in range(4) for c in range(2)])
REP = ("rep", [(0, 1), (1, 0)])


def send(values, route):
    return lax.ppermute(values, route[0], route[1])


def ring_gather(values, move):
    return [values, send(values, move(-1)), send(values, move(2)), send(values, move(1))]


def ring_gather_parts(values, move):
    up = send(values, move(-1))
    down = send(values, move(1))
    half = values.shape[0] // 2
    first = send(down[:half], move(1))
    second = send(up[half:], move(-1))
    return up, first, second, down


def ring_exchange(block_of, move):
    return [
        block_of(0),
        send(block_of(3), move(3)),
        send(block_of(2), move(2)),
        send(block_of(1), move(1)),
    ]


def ring_sum(block_of, move):
    arrived = [send(block_of(k).astype(BF16), move(k)) for k in (1, 2, 3)]
    total = block_of(0)
    for piece in arrived:
        total = total + piece.astype(F32)
    return total


NN = (((1,), (0,)), ((), ()))
NT = (((1,), (1,)), ((), ()))
TN = (((0,), (0,)), ((), ()))


def product(left, right, dims):
    return lax.dot_general(left, right, dims, preferred_element_type=F32)


def in_vmem():
    return pl.BlockSpec(memory_space=pltpu.VMEM)


def in_smem():
    return pl.BlockSpec(memory_space=pltpu.SMEM)


def anywhere():
    return pl.BlockSpec(memory_space=pl.ANY)


def fetch(sems, *pairs):
    copies = [
        pltpu.make_async_copy(source, target, sems.at[i])
        for i, (source, target) in enumerate(pairs)
    ]
    for copy in copies:
        copy.start()
    return copies


def call(kernel, operands, specs, outs, scratch=(), flops=0, mib=16):
    moved = sum(a.size * a.dtype.itemsize for a in operands)
    return pl.pallas_call(
        kernel,
        out_shape=[jax.ShapeDtypeStruct(shape, kind) for shape, kind in outs],
        in_specs=specs,
        out_specs=[in_vmem() for _ in outs],
        scratch_shapes=list(scratch),
        cost_estimate=pl.CostEstimate(flops=flops, bytes_accessed=moved, transcendentals=0),
        compiler_params=pltpu.CompilerParams(vmem_limit_bytes=mib * 1024 * 1024),
    )(*operands)


def unit_rows(values, gain):
    scale = lax.rsqrt(jnp.mean(values * values, axis=-1, keepdims=True) + 1e-06)
    return values * scale * gain


def pack_kernel(qkv_ref, low_ref, out_ref):
    width = qkv_ref.shape[2]
    for p in range(3):
        out_ref[:, p * width : (p + 1) * width] = qkv_ref[p]
    out_ref[:, 3 * width :] = low_ref[...]


def generator_kernel(at, latent_ref, gain_ref, up_ref, normed_ref, hidden_ref, slope_ref):
    for dz in range(4):
        for dc in range(2):
            block = lax.rem(at[2] + dz, 4) * 2 + lax.rem(at[3] + dc, 2)
            start = pl.multiple_of(block * 16, 16)
            values = latent_ref[pl.ds(start, 16), :].astype(F32)
            first = (dz * 2 + dc) * 16
            normed_ref[first : first + 16, :] = unit_rows(values, gain_ref[...]).astype(BF16)
    pre = product(normed_ref[...], up_ref[...], NT)
    curve = jnp.tanh(0.7978845608028654 * (pre + 0.044715 * (pre * pre * pre)))
    hidden_ref[...] = (0.5 * pre * (1.0 + curve)).astype(BF16)
    slope_ref[...] = 0.5 * (1.0 + curve) + 0.5 * pre * (1.0 - curve * curve) * (
        0.7978845608028654 * (1.0 + 0.134145 * (pre * pre))
    )


def update_kernel(hidden_ref, down_ref, own_ref, other_ref):
    update = product(hidden_ref[...], down_ref[...], NN)
    for dz in range(4):
        own_ref[dz] = update[dz * 32 : dz * 32 + 16]
        other_ref[dz] = update[dz * 32 + 16 : dz * 32 + 32].astype(BF16)


def strips_kernel(normed_ref, out_ref):
    for y in range(4):
        for x in range(4):
            out_ref[y, :, x * 160 : (x + 1) * 160] = normed_ref[
                :, x * 640 + y * 160 : x * 640 + (y + 1) * 160
            ]


def score_kernel(
    at, time, column_ref, other_ref, noise_ref, gain_ref,
    score_ref, sample_ref, noise_out, ordered_ref,
):
    for dz in range(4):
        for dc in range(2):
            block = lax.rem(at[2] + dz, 4) * 2 + lax.rem(at[3] + dc, 2)
            place = pl.ds(pl.multiple_of(block * 16, 16), 16)
            noise = noise_ref[place, :]
            sample = column_ref[dz] if dc == 0 else other_ref[dz]
            cut = slice((dz * 2 + dc) * 16, (dz * 2 + dc) * 16 + 16)
            sample_ref[cut, :] = sample
            ordered_ref[place, :] = sample
            noise_out[cut, :] = noise
            noisy = (1.0 - time[0]) * sample.astype(F32) + time[0] * noise.astype(F32)
            noisy = noisy.astype(BF16).astype(F32)
            score_ref[cut, :] = unit_rows(noisy, gain_ref[...]).astype(BF16)


def project_kernel(score_ref, up_ref, weight_ref, key_ref, value_ref, query_ref):
    result = product(score_ref[...], weight_ref[...], NN)
    width = key_ref.shape[1]
    query = result[:, :width]
    key_ref[...] = result[:, width : 2 * width].astype(BF16)
    value_ref[...] = result[:, 2 * width : 3 * width].astype(BF16)
    low = result[:, 3 * width :].astype(BF16)
    query_ref[:128] = query.astype(BF16)
    query_ref[128:] = (query + product(low, up_ref[...], NN)).astype(BF16)


def attention_kernel(query_ref, *rest):
    pieces, (real_ref, fake_ref, keys, values, sems) = rest[:10], rest[10:]
    width = query_ref.shape[1]
    pairs = []
    for which, target in ((0, keys), (1, values)):
        line, up, opp_a, opp_b, down = pieces[which * 5 : which * 5 + 5]
        for ref, first, count, distance in (
            (line, 0, 4, 0), (up, 0, 4, 1), (opp_a, 0, 2, 2), (opp_b, 2, 2, 2), (down, 0, 4, 3),
        ):
            if which == 0:
                start = (distance * 4 + first) * 128
                pairs.append((ref, target.at[pl.ds(start, count * 128)]))
            else:
                for i in range(count):
                    start = ((first + i) * 4 + distance) * 128
                    pairs.append(
                        (ref.at[pl.ds(i * 128, 128)], target.at[pl.ds(start, 128)])
                    )
    for copy in fetch(sems, *pairs):
        copy.wait()
    for which, mixed_ref in ((0, real_ref), (1, fake_ref)):
        for start in range(0, width, HEAD):
            cut = slice(start, start + HEAD)
            scores = product(
                query_ref[which * 128 : (which + 1) * 128, cut], keys[:, cut], NT
            ) * (HEAD ** (-0.5))
            weights = jnp.exp(scores - jnp.max(scores, axis=-1, keepdims=True))
            total = jnp.sum(weights, axis=-1, keepdims=True)
            mix = product(weights.astype(BF16), values[:, cut], NN) / total
            mixed_ref[:, cut] = mix.astype(BF16)


def output_kernel(real_ref, fake_ref, out_ref, down_ref, up_ref, own_ref, other_ref):
    real, fake = real_ref[...], fake_ref[...]
    out = out_ref[...]
    latent = product(fake, down_ref[...], NT)
    high = latent.astype(BF16)
    low = (latent - high.astype(F32)).astype(BF16)
    difference = (
        product(real, out, NT)
        - product(fake, out, NT)
        - (product(high, up_ref[...], NN) + product(low, up_ref[...], NN))
    )
    features = out_ref.shape[0]
    for dz in range(4):
        cut = slice(dz * 32, dz * 32 + 16)
        own_ref[dz, :, :features] = difference[cut]
        own_ref[dz, :, features:] = latent[cut]
        cut = slice(dz * 32 + 16, dz * 32 + 32)
        other_ref[dz, :, :features] = difference[cut].astype(BF16)
        other_ref[dz, :, features:] = latent[cut].astype(BF16)


def backward_kernel(
    column_hbm, other_hbm, down_ref, slope_ref, fake_ref, sample_ref, noise_ref,
    pre_ref, quarters_ref, both, whole, wide, sems,
):
    for copy in fetch(sems, (column_hbm, both.at[0]), (other_hbm, both.at[1])):
        copy.wait()
    features = down_ref.shape[1]
    quarter = features // 4
    for dz in range(4):
        for dc in range(2):
            cut = slice((dz * 2 + dc) * 16, (dz * 2 + dc) * 16 + 16)
            whole[cut, :] = both[dc, dz]
    for x in range(4):
        quarters_ref[x, :128, :] = whole[:, x * quarter : (x + 1) * quarter]
    latent = whole[:, features:]
    width, share, depth = fake_ref.shape[1], sample_ref.shape[1], latent.shape[1]
    error = sample_ref[...].astype(F32) - noise_ref[...].astype(F32)
    high = error.astype(BF16)
    wide[:, :width] = product(latent, fake_ref[...], TN)
    wide[:, width : width + share] = product(latent, high, TN) + product(
        latent, (error - high.astype(F32)).astype(BF16), TN
    )
    wide[:, width + share :] = product(latent, latent, TN)
    for x in range(4):
        quarters_ref[x, 128:144, :] = wide[x * 16 : x * 16 + 16, :quarter].astype(BF16)
        quarters_ref[x, 144:160, :] = jnp.zeros((16, quarter), BF16)
        quarters_ref[x, 144:160, : width + share + depth - quarter] = wide[
            x * 16 : x * 16 + 16, quarter:
        ].astype(BF16)
    grad = product(whole[:, :features], down_ref[...], NT)
    pre_ref[...] = (grad * slope_ref[...]).astype(BF16)


def join_kernel(*refs):
    for ref, first in ((refs[8], 0), (refs[9], 4)):
        rows = refs[first].shape[0]
        for i in range(4):
            ref[i * rows : (i + 1) * rows, :] = refs[first + i][...]


def term_kernel(at, hidden_ref, normed_ref, *rest):
    cotangents, pres = rest[:4], rest[4:8]
    down_outs, up_outs, (term,) = rest[8:12], rest[12:16], rest[16:]
    rows = jnp.concatenate([ref[:128, :] for ref in cotangents])
    term[...] = product(rows, hidden_ref[...], TN)
    for k in range(4):
        start = pl.multiple_of(lax.rem(at[1] + k, 4) * 160, 16)
        down_outs[k][:160, :] = term[pl.ds(start, 160), :].astype(down_outs[k].dtype)
    term[...] = product(normed_ref[...], jnp.concatenate([ref[...] for ref in pres]), TN)
    for k in range(4):
        start = pl.multiple_of(lax.rem(at[0] + k, 4) * 160, 16)
        up_outs[k][...] = term[pl.ds(start, 160), :].astype(up_outs[k].dtype)
    extra = cotangents[0][128:, :].astype(F32)
    for ref in cotangents[1:]:
        extra = extra + ref[128:, :].astype(F32)
    for ref in down_outs:
        ref[160:, :] = jnp.zeros((16, ref.shape[1]), ref.dtype)
        ref[160:, :640] = extra[:16].astype(ref.dtype)
        ref[160:, 640:768] = extra[16:, :128].astype(ref.dtype)


def moments_kernel(moments_ref, out_ref, strips_ref):
    width = 3 * HEAD
    out = out_ref[...]
    rows = moments_ref[:, :width]
    high = rows.astype(BF16)
    low = (rows - high.astype(F32)).astype(BF16)
    through = product(high, out, NT) + product(low, out, NT)
    for g in range(8):
        strips_ref[g] = through[:, g * 320 : (g + 1) * 320]


def group_sum(own, other):
    pair = own + send(other, CORE).astype(F32)
    return ring_sum(lambda k: pair[k], move_z)


def group_gather(rows):
    column = jnp.stack(ring_gather(rows, move_z))
    return column, send(column, CORE)


def spread(values, first_move, second_move):
    up, opp_a, opp_b, down = ring_gather_parts(values, first_move)
    line = jnp.concatenate([values, up, opp_a, opp_b, down])
    return (line,) + ring_gather_parts(line, second_move)


def split_bf16(values):
    high = values.astype(BF16)
    return jnp.concatenate([high, (values - high.astype(F32)).astype(BF16)])


def shards(
    latents,
    noise_draw,
    timesteps,
    gen_gain,
    up_weight,
    down_weight,
    score_gain,
    qkv_weight,
    out_weight,
    query_down,
    query_up,
    output_down,
    output_up,
):
    place = lax.axis_index("seq")
    at_x, at_y = place // 4, place % 4
    group = lax.axis_index("grp")
    at_z, at_core = group // 2, group % 2
    at_rep = lax.axis_index("rep")
    at = jnp.stack([at_x, at_y, at_z, at_core]).astype(jnp.int32)
    clip_time = timesteps[0]
    rows, width = latents.shape[1:]
    units = up_weight.shape[1]
    share = width // 8
    head_width = out_weight.shape[1]
    depth = query_down.shape[1]
    vm, sm, hb = in_vmem(), in_smem(), anywhere()


    def pick(values, index):
        return lax.dynamic_index_in_dim(values, index % 4, 0, keepdims=False)

    vector_rows = qkv_weight.shape[0]
    (own_weight,) = call(
        pack_kernel,
        (qkv_weight.transpose(1, 0, 2), query_down),
        [vm, vm],
        [((vector_rows, 3 * head_width + depth), BF16)],
        mib=8,
    )
    score_weight = lax.all_gather(own_weight, "seq", axis=0, tiled=True)
    columns = score_weight.shape[1]

    up_rows, down_rows = up_weight.T, down_weight.T
    normed, hidden, slope = call(
        generator_kernel,
        (at, latents[0], gen_gain[None], up_rows),
        [sm, vm, vm, vm],
        [((rows, width), BF16), ((rows, units), BF16), ((rows, units), F32)],
        flops=2 * rows * width * units,
        mib=12,
    )
    own, other = call(
        update_kernel,
        (hidden, down_rows),
        [vm, vm],
        [((4, 16, width), F32), ((4, 16, width), BF16)],
        flops=2 * rows * width * units,
        mib=12,
    )
    (strips,) = call(strips_kernel, (normed,), [vm], [((4, rows, width // 4), BF16)])
    update = group_sum(own, other)
    update, late_out = lax.optimization_barrier((update, out_weight))
    out_rows = lax.all_gather(late_out, "seq", axis=0, tiled=True)
    latent_own = lax.dynamic_slice_in_dim(latents[0], group * 16, 16, 0)
    column, other = group_gather((latent_own.astype(F32) + update).astype(BF16))

    score_in, sample, noise_rows, ordered = call(
        score_kernel,
        (at, timesteps, column, other, noise_draw[0], score_gain[None]),
        [sm, sm, vm, vm, vm, vm],
        [((rows, width), BF16)] * 4,
    )
    sample_out = lax.dynamic_slice_in_dim(ordered, group * share, share, 1)
    sample_share = lax.dynamic_slice_in_dim(sample, group * share, share, 1)
    noise_share = lax.dynamic_slice_in_dim(noise_rows, group * share, share, 1)

    score_in, sample_out, sample_share, noise_share = lax.optimization_barrier(
        (score_in, sample_out, sample_share, noise_share)
    )
    key_rows, value_rows, queries = call(
        project_kernel,
        (score_in, query_up, score_weight),
        [vm, vm, vm],
        [((rows, head_width), BF16), ((rows, head_width), BF16), ((2 * rows, head_width), BF16)],
        flops=2 * rows * width * columns,
    )

    queries, hidden, strips = lax.optimization_barrier((queries, hidden, strips))

    key_pieces = spread(key_rows, move_x, move_y)
    value_pieces = spread(value_rows, move_y, move_x)
    mixed_real, mixed_fake = call(
        attention_kernel,
        (queries,) + key_pieces + value_pieces,
        [vm] + [hb] * 10,
        [((rows, head_width), BF16)] * 2,
        [pltpu.VMEM((16 * rows, head_width), BF16)] * 2 + [pltpu.SemaphoreType.DMA((21,))],
        flops=16 * rows * rows * 16 * head_width,
    )
    own, other = call(
        output_kernel,
        (mixed_real, mixed_fake, out_rows, output_down.T, output_up),
        [vm] * 5,
        [((4, 16, width + depth), F32), ((4, 16, width + depth), BF16)],
        flops=4 * rows * width * head_width,
    )
    hidden_line = ring_gather(hidden, move_x)
    normed_line = ring_exchange(lambda k: pick(strips, at_y + k), move_y)
    hidden_line, normed_line = call(
        join_kernel,
        tuple(hidden_line) + tuple(normed_line),
        [vm] * 8,
        [((4 * rows, units), BF16), ((4 * rows, width // 4), BF16)],
        mib=8,
    )
    own, other, hidden_line, normed_line = lax.optimization_barrier(
        (own, other, hidden_line, normed_line)
    )
    summed = group_sum(own, other)
    column, other = group_gather(
        jnp.concatenate([clip_time * summed[:, :width], summed[:, width:]], axis=1).astype(BF16)
    )
    pre_grad, quarters = call(
        backward_kernel,
        (column, other, down_rows, slope, mixed_fake, sample_share, noise_share),
        [hb] * 2 + [vm] * 5,
        [((rows, units), BF16), ((4, rows + 32, width // 4), BF16)],
        [
            pltpu.VMEM((2, 4, 16, width + depth), BF16),
            pltpu.VMEM((rows, width + depth), BF16),
            pltpu.VMEM((depth, head_width + share + depth), F32),
            pltpu.SemaphoreType.DMA((2,)),
        ],
        flops=2 * rows * width * units,
    )

    part = width // 16

    def rep_sum(total):
        half = total.shape[0] // 2
        kept = lax.dynamic_slice_in_dim(total, at_rep * half, half, 0)
        given = lax.dynamic_slice_in_dim(total, (1 - at_rep) * half, half, 0)
        return kept + send(given.astype(BF16), REP).astype(F32)

    cotangent_line = ring_exchange(lambda k: pick(quarters, at_x + k), move_x)
    pre_line = ring_gather(pre_grad, move_y)
    blocks = call(
        term_kernel,
        (at, hidden_line, normed_line) + tuple(cotangent_line) + tuple(pre_line),
        [sm] + [vm] * 10,
        [((part + 16, units), F32)]
        + [((part + 16, units), BF16)] * 3
        + [((part, units), F32)]
        + [((part, units), BF16)] * 3,
        [pltpu.VMEM((width // 4, units), F32)],
        flops=4 * rows * width * units,
        mib=20,
    )
    down_arrived = [send(blocks[k], move_y(k)) for k in (1, 2, 3)]
    up_arrived = [send(blocks[4 + k], move_x(k)) for k in (1, 2, 3)]
    down_total, up_total = blocks[0], blocks[4]
    for k in range(3):
        down_total = down_total + down_arrived[k].astype(F32)
        up_total = up_total + up_arrived[k].astype(F32)

    down_weight_gradient = rep_sum(down_total[:part])
    up_weight_gradient = rep_sum(up_total)

    moments = down_total[part:, : head_width + share + depth]
    (out_strips,) = call(
        moments_kernel,
        (moments, out_rows),
        [vm, vm],
        [((8, 16, share), F32)],
        flops=64 * width * head_width,
    )
    moments = lax.dynamic_slice_in_dim(moments, at_y * 4, 4, 0)
    out_strips = lax.dynamic_slice_in_dim(out_strips, at_y * 4, 4, 1).reshape(4, 2, 4, share)
    other = lax.dynamic_index_in_dim(out_strips, 1 - at_core, 1, keepdims=False)
    pair = lax.dynamic_index_in_dim(out_strips, at_core, 1, keepdims=False)
    pair = pair + send(other.astype(BF16), CORE).astype(F32)
    through_out = ring_sum(lambda k: pick(pair, at_z + k), move_z)
    up_share = lax.dynamic_slice_in_dim(output_up, group * share, share, 1)
    through_up = product(split_bf16(moments[:, head_width + share :]), up_share, NN)
    adapter_up_gradient = rep_sum(
        through_out
        + moments[:, head_width : head_width + share]
        + through_up[:4]
        + through_up[4:]
    )
    return (sample_out[None], up_weight_gradient, down_weight_gradient, adapter_up_gradient)


def solution(mesh):
    in_specs = (
        P("rep", "seq", None),
        P("rep", "seq", None),
        P("rep"),
        P(),
        P(None, "grp"),
        P(None, "grp"),
        P(),
        P("seq", None, "grp"),
        P("seq", "grp"),
        P("seq", None),
        P(None, "grp"),
        P("grp", None),
        P(),
    )
    out_specs = (
        P("rep", "seq", "grp"),
        P(("seq", "rep"), "grp"),
        P(("seq", "rep"), "grp"),
        P(("seq", "rep"), "grp"),
    )
    return jax.shard_map(shards, mesh=mesh, in_specs=in_specs, out_specs=out_specs, check_vma=False)
```

```python
import jax
import jax.numpy as jnp
from jax import lax
from jax.experimental import pallas as pl
from jax.experimental.pallas import tpu as pltpu
from jax.sharding import PartitionSpec as P

HEAD = 128
F32 = jnp.float32
BF16 = jnp.bfloat16


def move_x(d):
    return "seq", [(x * 4 + y, ((x + d) % 4) * 4 + y) for x in range(4) for y in range(4)]


def move_y(d):
    return "seq", [(x * 4 + y, x * 4 + (y + d) % 4) for x in range(4) for y in range(4)]


def move_z(d):
    return "grp", [(z * 2 + c, ((z + d) % 4) * 2 + c) for z in range(4) for c in range(2)]


CORE = ("grp", [(z * 2 + c, z * 2 + 1 - c) for z in range(4) for c in range(2)])
REP = ("rep", [(0, 1), (1, 0)])


def send(values, route):
    return lax.ppermute(values, route[0], route[1])


def ring_gather(values, move):
    return [values, send(values, move(-1)), send(values, move(2)), send(values, move(1))]


def ring_gather_parts(values, move):
    up = send(values, move(-1))
    down = send(values, move(1))
    half = values.shape[0] // 2
    first = send(down[:half], move(1))
    second = send(up[half:], move(-1))
    return up, first, second, down


def ring_exchange(block_of, move):
    return [
        block_of(0),
        send(block_of(3), move(3)),
        send(block_of(2), move(2)),
        send(block_of(1), move(1)),
    ]


def ring_sum(block_of, move):
    arrived = [send(block_of(k).astype(BF16), move(k)) for k in (1, 2, 3)]
    total = block_of(0)
    for piece in arrived:
        total = total + piece.astype(F32)
    return total


NN = (((1,), (0,)), ((), ()))
NT = (((1,), (1,)), ((), ()))
TN = (((0,), (0,)), ((), ()))


def product(left, right, dims):
    return lax.dot_general(left, right, dims, preferred_element_type=F32)


def in_vmem():
    return pl.BlockSpec(memory_space=pltpu.VMEM)


def in_smem():
    return pl.BlockSpec(memory_space=pltpu.SMEM)


def anywhere():
    return pl.BlockSpec(memory_space=pl.ANY)


def fetch(sems, *pairs):
    copies = [
        pltpu.make_async_copy(source, target, sems.at[i])
        for i, (source, target) in enumerate(pairs)
    ]
    for copy in copies:
        copy.start()
    return copies


def call(kernel, operands, specs, outs, scratch=(), flops=0, mib=16):
    moved = sum(a.size * a.dtype.itemsize for a in operands)
    return pl.pallas_call(
        kernel,
        out_shape=[jax.ShapeDtypeStruct(shape, kind) for shape, kind in outs],
        in_specs=specs,
        out_specs=[in_vmem() for _ in outs],
        scratch_shapes=list(scratch),
        cost_estimate=pl.CostEstimate(flops=flops, bytes_accessed=moved, transcendentals=0),
        compiler_params=pltpu.CompilerParams(vmem_limit_bytes=mib * 1024 * 1024),
    )(*operands)


def unit_rows(values, gain):
    scale = lax.rsqrt(jnp.mean(values * values, axis=-1, keepdims=True) + 1e-06)
    return values * scale * gain


def pack_kernel(qkv_ref, low_ref, out_ref):
    width = qkv_ref.shape[2]
    for p in range(3):
        out_ref[:, p * width : (p + 1) * width] = qkv_ref[p]
    out_ref[:, 3 * width :] = low_ref[...]


def generator_kernel(at, latent_ref, gain_ref, up_ref, normed_ref, hidden_ref, slope_ref):
    for dz in range(4):
        for dc in range(2):
            block = lax.rem(at[2] + dz, 4) * 2 + lax.rem(at[3] + dc, 2)
            start = pl.multiple_of(block * 16, 16)
            values = latent_ref[pl.ds(start, 16), :].astype(F32)
            first = (dz * 2 + dc) * 16
            normed_ref[first : first + 16, :] = unit_rows(values, gain_ref[...]).astype(BF16)
    pre = product(normed_ref[...], up_ref[...], NT)
    curve = jnp.tanh(0.7978845608028654 * (pre + 0.044715 * (pre * pre * pre)))
    hidden_ref[...] = (0.5 * pre * (1.0 + curve)).astype(BF16)
    slope_ref[...] = 0.5 * (1.0 + curve) + 0.5 * pre * (1.0 - curve * curve) * (
        0.7978845608028654 * (1.0 + 0.134145 * (pre * pre))
    )


def update_kernel(hidden_ref, down_ref, own_ref, other_ref):
    update = product(hidden_ref[...], down_ref[...], NN)
    for dz in range(4):
        own_ref[dz] = update[dz * 32 : dz * 32 + 16]
        other_ref[dz] = update[dz * 32 + 16 : dz * 32 + 32].astype(BF16)


def strips_kernel(normed_ref, out_ref):
    for y in range(4):
        for x in range(4):
            out_ref[y, :, x * 160 : (x + 1) * 160] = normed_ref[
                :, x * 640 + y * 160 : x * 640 + (y + 1) * 160
            ]


def score_kernel(
    at, time, column_ref, other_ref, noise_ref, gain_ref,
    score_ref, sample_ref, noise_out, ordered_ref,
):
    for dz in range(4):
        for dc in range(2):
            block = lax.rem(at[2] + dz, 4) * 2 + lax.rem(at[3] + dc, 2)
            place = pl.ds(pl.multiple_of(block * 16, 16), 16)
            noise = noise_ref[place, :]
            sample = column_ref[dz] if dc == 0 else other_ref[dz]
            cut = slice((dz * 2 + dc) * 16, (dz * 2 + dc) * 16 + 16)
            sample_ref[cut, :] = sample
            ordered_ref[place, :] = sample
            noise_out[cut, :] = noise
            noisy = (1.0 - time[0]) * sample.astype(F32) + time[0] * noise.astype(F32)
            noisy = noisy.astype(BF16).astype(F32)
            score_ref[cut, :] = unit_rows(noisy, gain_ref[...]).astype(BF16)


def project_kernel(score_ref, up_ref, weight_ref, key_ref, value_ref, query_ref):
    result = product(score_ref[...], weight_ref[...], NN)
    width = key_ref.shape[1]
    query = result[:, :width]
    key_ref[...] = result[:, width : 2 * width].astype(BF16)
    value_ref[...] = result[:, 2 * width : 3 * width].astype(BF16)
    low = result[:, 3 * width :].astype(BF16)
    query_ref[:128] = query.astype(BF16)
    query_ref[128:] = (query + product(low, up_ref[...], NN)).astype(BF16)


def attention_kernel(query_ref, *rest):
    pieces, (real_ref, fake_ref, keys, values, sems) = rest[:10], rest[10:]
    width = query_ref.shape[1]
    pairs = []
    for which, target in ((0, keys), (1, values)):
        line, up, opp_a, opp_b, down = pieces[which * 5 : which * 5 + 5]
        for ref, first, count, distance in (
            (line, 0, 4, 0), (up, 0, 4, 1), (opp_a, 0, 2, 2), (opp_b, 2, 2, 2), (down, 0, 4, 3),
        ):
            if which == 0:
                start = (distance * 4 + first) * 128
                pairs.append((ref, target.at[pl.ds(start, count * 128)]))
            else:
                for i in range(count):
                    start = ((first + i) * 4 + distance) * 128
                    pairs.append(
                        (ref.at[pl.ds(i * 128, 128)], target.at[pl.ds(start, 128)])
                    )
    for copy in fetch(sems, *pairs):
        copy.wait()
    for which, mixed_ref in ((0, real_ref), (1, fake_ref)):
        for start in range(0, width, HEAD):
            cut = slice(start, start + HEAD)
            scores = product(
                query_ref[which * 128 : (which + 1) * 128, cut], keys[:, cut], NT
            ) * (HEAD ** (-0.5))
            weights = jnp.exp(scores - jnp.max(scores, axis=-1, keepdims=True))
            total = jnp.sum(weights, axis=-1, keepdims=True)
            mix = product(weights.astype(BF16), values[:, cut], NN) / total
            mixed_ref[:, cut] = mix.astype(BF16)


def output_kernel(real_ref, fake_ref, out_ref, down_ref, up_ref, own_ref, other_ref):
    real, fake = real_ref[...], fake_ref[...]
    out = out_ref[...]
    latent = product(fake, down_ref[...], NT)
    high = latent.astype(BF16)
    low = (latent - high.astype(F32)).astype(BF16)
    difference = (
        product(real, out, NT)
        - product(fake, out, NT)
        - (product(high, up_ref[...], NN) + product(low, up_ref[...], NN))
    )
    features = out_ref.shape[0]
    for dz in range(4):
        cut = slice(dz * 32, dz * 32 + 16)
        own_ref[dz, :, :features] = difference[cut]
        own_ref[dz, :, features:] = latent[cut]
        cut = slice(dz * 32 + 16, dz * 32 + 32)
        other_ref[dz, :, :features] = difference[cut].astype(BF16)
        other_ref[dz, :, features:] = latent[cut].astype(BF16)


def backward_kernel(
    column_hbm, other_hbm, down_ref, slope_ref, fake_ref, sample_ref, noise_ref,
    pre_ref, quarters_ref, both, whole, wide, sems,
):
    for copy in fetch(sems, (column_hbm, both.at[0]), (other_hbm, both.at[1])):
        copy.wait()
    features = down_ref.shape[1]
    quarter = features // 4
    for dz in range(4):
        for dc in range(2):
            cut = slice((dz * 2 + dc) * 16, (dz * 2 + dc) * 16 + 16)
            whole[cut, :] = both[dc, dz]
    for x in range(4):
        quarters_ref[x, :128, :] = whole[:, x * quarter : (x + 1) * quarter]
    latent = whole[:, features:]
    width, share, depth = fake_ref.shape[1], sample_ref.shape[1], latent.shape[1]
    error = sample_ref[...].astype(F32) - noise_ref[...].astype(F32)
    high = error.astype(BF16)
    wide[:, :width] = product(latent, fake_ref[...], TN)
    wide[:, width : width + share] = product(latent, high, TN) + product(
        latent, (error - high.astype(F32)).astype(BF16), TN
    )
    wide[:, width + share :] = product(latent, latent, TN)
    for x in range(4):
        quarters_ref[x, 128:144, :] = wide[x * 16 : x * 16 + 16, :quarter].astype(BF16)
        quarters_ref[x, 144:160, :] = jnp.zeros((16, quarter), BF16)
        quarters_ref[x, 144:160, : width + share + depth - quarter] = wide[
            x * 16 : x * 16 + 16, quarter:
        ].astype(BF16)
    grad = product(whole[:, :features], down_ref[...], NT)
    pre_ref[...] = (grad * slope_ref[...]).astype(BF16)


def join_kernel(*refs):
    for ref, first in ((refs[8], 0), (refs[9], 4)):
        rows = refs[first].shape[0]
        for i in range(4):
            ref[i * rows : (i + 1) * rows, :] = refs[first + i][...]


def term_kernel(at, hidden_ref, normed_ref, *rest):
    cotangents, pres = rest[:4], rest[4:8]
    down_outs, up_outs, (term,) = rest[8:12], rest[12:16], rest[16:]
    rows = jnp.concatenate([ref[:128, :] for ref in cotangents])
    term[...] = product(rows, hidden_ref[...], TN)
    for k in range(4):
        start = pl.multiple_of(lax.rem(at[1] + k, 4) * 160, 16)
        down_outs[k][:160, :] = term[pl.ds(start, 160), :].astype(down_outs[k].dtype)
    term[...] = product(normed_ref[...], jnp.concatenate([ref[...] for ref in pres]), TN)
    for k in range(4):
        start = pl.multiple_of(lax.rem(at[0] + k, 4) * 160, 16)
        up_outs[k][...] = term[pl.ds(start, 160), :].astype(up_outs[k].dtype)
    extra = cotangents[0][128:, :].astype(F32)
    for ref in cotangents[1:]:
        extra = extra + ref[128:, :].astype(F32)
    for ref in down_outs:
        ref[160:, :] = jnp.zeros((16, ref.shape[1]), ref.dtype)
        ref[160:, :640] = extra[:16].astype(ref.dtype)
        ref[160:, 640:768] = extra[16:, :128].astype(ref.dtype)


def moments_kernel(moments_ref, out_ref, strips_ref):
    width = 3 * HEAD
    out = out_ref[...]
    rows = moments_ref[:, :width]
    high = rows.astype(BF16)
    low = (rows - high.astype(F32)).astype(BF16)
    through = product(high, out, NT) + product(low, out, NT)
    for g in range(8):
        strips_ref[g] = through[:, g * 320 : (g + 1) * 320]


def group_sum(own, other):
    pair = own + send(other, CORE).astype(F32)
    return ring_sum(lambda k: pair[k], move_z)


def group_gather(rows):
    column = jnp.stack(ring_gather(rows, move_z))
    return column, send(column, CORE)


def spread(values, first_move, second_move):
    up, opp_a, opp_b, down = ring_gather_parts(values, first_move)
    line = jnp.concatenate([values, up, opp_a, opp_b, down])
    return (line,) + ring_gather_parts(line, second_move)


def split_bf16(values):
    high = values.astype(BF16)
    return jnp.concatenate([high, (values - high.astype(F32)).astype(BF16)])


def shards(
    latents,
    noise_draw,
    timesteps,
    gen_gain,
    up_weight,
    down_weight,
    score_gain,
    qkv_weight,
    out_weight,
    query_down,
    query_up,
    output_down,
    output_up,
):
    place = lax.axis_index("seq")
    at_x, at_y = place // 4, place % 4
    group = lax.axis_index("grp")
    at_z, at_core = group // 2, group % 2
    at_rep = lax.axis_index("rep")
    at = jnp.stack([at_x, at_y, at_z, at_core]).astype(jnp.int32)
    clip_time = timesteps[0]
    rows, width = latents.shape[1:]
    units = up_weight.shape[1]
    share = width // 8
    head_width = out_weight.shape[1]
    depth = query_down.shape[1]
    vm, sm, hb = in_vmem(), in_smem(), anywhere()


    def pick(values, index):
        return lax.dynamic_index_in_dim(values, index % 4, 0, keepdims=False)

    vector_rows = qkv_weight.shape[0]
    (own_weight,) = call(
        pack_kernel,
        (qkv_weight.transpose(1, 0, 2), query_down),
        [vm, vm],
        [((vector_rows, 3 * head_width + depth), BF16)],
        mib=8,
    )
    score_weight = lax.all_gather(own_weight, "seq", axis=0, tiled=True)
    columns = score_weight.shape[1]

    up_rows, down_rows = up_weight.T, down_weight.T
    normed, hidden, slope = call(
        generator_kernel,
        (at, latents[0], gen_gain[None], up_rows),
        [sm, vm, vm, vm],
        [((rows, width), BF16), ((rows, units), BF16), ((rows, units), F32)],
        flops=2 * rows * width * units,
        mib=12,
    )
    own, other = call(
        update_kernel,
        (hidden, down_rows),
        [vm, vm],
        [((4, 16, width), F32), ((4, 16, width), BF16)],
        flops=2 * rows * width * units,
        mib=12,
    )
    (strips,) = call(strips_kernel, (normed,), [vm], [((4, rows, width // 4), BF16)])
    update = group_sum(own, other)
    update, late_hidden, strips, late_out = lax.optimization_barrier(
        (update, hidden, strips, out_weight)
    )
    out_rows = lax.all_gather(late_out, "seq", axis=0, tiled=True)
    after, first, second, before = ring_gather_parts(late_hidden, move_x)
    hidden_line = [late_hidden, after, jnp.concatenate([first, second]), before]
    normed_line = ring_exchange(lambda k: pick(strips, at_y + k), move_y)
    latent_own = lax.dynamic_slice_in_dim(latents[0], group * 16, 16, 0)
    column, other = group_gather((latent_own.astype(F32) + update).astype(BF16))

    score_in, sample, noise_rows, ordered = call(
        score_kernel,
        (at, timesteps, column, other, noise_draw[0], score_gain[None]),
        [sm, sm, vm, vm, vm, vm],
        [((rows, width), BF16)] * 4,
    )
    sample_out = lax.dynamic_slice_in_dim(ordered, group * share, share, 1)
    sample_share = lax.dynamic_slice_in_dim(sample, group * share, share, 1)
    noise_share = lax.dynamic_slice_in_dim(noise_rows, group * share, share, 1)

    hidden_line, normed_line = call(
        join_kernel,
        tuple(hidden_line) + tuple(normed_line),
        [vm] * 8,
        [((4 * rows, units), BF16), ((4 * rows, width // 4), BF16)],
        mib=8,
    )
    score_in, hidden_line, normed_line, sample_out, sample_share, noise_share = (
        lax.optimization_barrier(
            (score_in, hidden_line, normed_line, sample_out, sample_share, noise_share)
        )
    )
    key_rows, value_rows, queries = call(
        project_kernel,
        (score_in, query_up, score_weight),
        [vm, vm, vm],
        [((rows, head_width), BF16), ((rows, head_width), BF16), ((2 * rows, head_width), BF16)],
        flops=2 * rows * width * columns,
    )

    key_pieces = spread(key_rows, move_x, move_y)
    value_pieces = spread(value_rows, move_y, move_x)
    mixed_real, mixed_fake = call(
        attention_kernel,
        (queries,) + key_pieces + value_pieces,
        [vm] + [hb] * 10,
        [((rows, head_width), BF16)] * 2,
        [pltpu.VMEM((16 * rows, head_width), BF16)] * 2 + [pltpu.SemaphoreType.DMA((21,))],
        flops=16 * rows * rows * 16 * head_width,
    )
    own, other = call(
        output_kernel,
        (mixed_real, mixed_fake, out_rows, output_down.T, output_up),
        [vm] * 5,
        [((4, 16, width + depth), F32), ((4, 16, width + depth), BF16)],
        flops=4 * rows * width * head_width,
    )
    summed = group_sum(own, other)
    column, other = group_gather(
        jnp.concatenate([clip_time * summed[:, :width], summed[:, width:]], axis=1).astype(BF16)
    )
    pre_grad, quarters = call(
        backward_kernel,
        (column, other, down_rows, slope, mixed_fake, sample_share, noise_share),
        [hb] * 2 + [vm] * 5,
        [((rows, units), BF16), ((4, rows + 32, width // 4), BF16)],
        [
            pltpu.VMEM((2, 4, 16, width + depth), BF16),
            pltpu.VMEM((rows, width + depth), BF16),
            pltpu.VMEM((depth, head_width + share + depth), F32),
            pltpu.SemaphoreType.DMA((2,)),
        ],
        flops=2 * rows * width * units,
    )

    part = width // 16

    def rep_sum(total):
        half = total.shape[0] // 2
        kept = lax.dynamic_slice_in_dim(total, at_rep * half, half, 0)
        given = lax.dynamic_slice_in_dim(total, (1 - at_rep) * half, half, 0)
        return kept + send(given.astype(BF16), REP).astype(F32)

    cotangent_line = ring_exchange(lambda k: pick(quarters, at_x + k), move_x)
    pre_line = ring_gather(pre_grad, move_y)
    blocks = call(
        term_kernel,
        (at, hidden_line, normed_line) + tuple(cotangent_line) + tuple(pre_line),
        [sm] + [vm] * 10,
        [((part + 16, units), F32)]
        + [((part + 16, units), BF16)] * 3
        + [((part, units), F32)]
        + [((part, units), BF16)] * 3,
        [pltpu.VMEM((width // 4, units), F32)],
        flops=4 * rows * width * units,
        mib=20,
    )
    down_arrived = [send(blocks[k], move_y(k)) for k in (1, 2, 3)]
    up_arrived = [send(blocks[4 + k], move_x(k)) for k in (1, 2, 3)]
    down_total, up_total = blocks[0], blocks[4]
    for k in range(3):
        down_total = down_total + down_arrived[k].astype(F32)
        up_total = up_total + up_arrived[k].astype(F32)

    down_weight_gradient = rep_sum(down_total[:part])
    up_weight_gradient = rep_sum(up_total)

    moments = down_total[part:, : head_width + share + depth]
    (out_strips,) = call(
        moments_kernel,
        (moments, out_rows),
        [vm, vm],
        [((8, 16, share), F32)],
        flops=64 * width * head_width,
    )
    moments = lax.dynamic_slice_in_dim(moments, at_y * 4, 4, 0)
    out_strips = lax.dynamic_slice_in_dim(out_strips, at_y * 4, 4, 1).reshape(4, 2, 4, share)
    other = lax.dynamic_index_in_dim(out_strips, 1 - at_core, 1, keepdims=False)
    pair = lax.dynamic_index_in_dim(out_strips, at_core, 1, keepdims=False)
    pair = pair + send(other.astype(BF16), CORE).astype(F32)
    through_out = ring_sum(lambda k: pick(pair, at_z + k), move_z)
    up_share = lax.dynamic_slice_in_dim(output_up, group * share, share, 1)
    through_up = product(split_bf16(moments[:, head_width + share :]), up_share, NN)
    adapter_up_gradient = rep_sum(
        through_out
        + moments[:, head_width : head_width + share]
        + through_up[:4]
        + through_up[4:]
    )
    return (sample_out[None], up_weight_gradient, down_weight_gradient, adapter_up_gradient)


def solution(mesh):
    in_specs = (
        P("rep", "seq", None),
        P("rep", "seq", None),
        P("rep"),
        P(),
        P(None, "grp"),
        P(None, "grp"),
        P(),
        P("seq", None, "grp"),
        P("seq", "grp"),
        P("seq", None),
        P(None, "grp"),
        P("grp", None),
        P(),
    )
    out_specs = (
        P("rep", "seq", "grp"),
        P(("seq", "rep"), "grp"),
        P(("seq", "rep"), "grp"),
        P(("seq", "rep"), "grp"),
    )
    return jax.shard_map(shards, mesh=mesh, in_specs=in_specs, out_specs=out_specs, check_vma=False)
```
